128 devices in a mesh: expert: 64 (over z, y, x), tensor: 2 (over core).
Axes of the slice: x: 4, y: 4, z: 4, core: 2. Of those that a mesh axis runs over, the one named last changes fastest.
Arguments:
- tokens: bfloat16 [2048, 4096], P('expert', 'tensor'), may hold values from -6 to 6
- route_ids: int32 [2048, 8], P('expert'), may hold values from 0 to 63, all different within a row; in each aligned block of 32 rows (0 to 31, 32 to 63, ...) at most 8 rows name the same one
- route_weight: float32 [2048, 8], P('expert'), may hold values from 0.05 to 0.5
- gate_weight: bfloat16 [64, 768, 4096], P('expert', 'tensor'), may hold values from -0.09375 to 0.09375
- up_weight: bfloat16 [64, 768, 4096], P('expert', 'tensor'), may hold values from -0.09375 to 0.09375
- down_weight: bfloat16 [64, 768, 4096], P('expert', 'tensor'), may hold values from -0.21875 to 0.21875
- out_grad: bfloat16 [2048, 4096], P('expert', 'tensor'), may hold values from -6 to 6
Outputs:
- mixed: bfloat16 [2048, 4096], P('expert', 'tensor')
- tokens_grad: bfloat16 [2048, 4096], P('expert', 'tensor')
- route_grad: float32 [2048, 8], P('expert')
- gate_grad: bfloat16 [64, 768, 4096], P('expert', 'tensor')
- up_grad: bfloat16 [64, 768, 4096], P('expert', 'tensor')
- down_grad: bfloat16 [64, 768, 4096], P('expert', 'tensor')
The draws below stay inside these ranges and needn't reach their ends.
Inputs may be any that keep to these rules, and one draw needn't show every extreme that they name: `route_ids`: each row names 8 different experts. Within each aligned block of 32 rows (the tokens of one index of expert) no expert is named by more than 8 rows.
All inputs are finite; a program needn't handle non-finite values.
Results may differ from the reference program's by a relative error of at most 0.015.
Values may be sent and summed in bfloat16 or wider, within the bound.
A program may use at most 128 MiB of HBM per device.

```python
import math
import jax
import jax.numpy as jnp
import numpy as np
from jax import lax

D = 4096
FF = 768
TOP = 8
TOK_DEV = 32
EXPERTS = 64
TOKENS = 2048
CAP = 8
SLOTS = 512
N_EXPERT = 64
N_TENSOR = 2


def steps_of(stream_key, extent, shards, low, largest):
    gain = 1.0
    for dim, parts in shards:
        steps = jax.random.uniform(jax.random.fold_in(jax.random.fold_in(stream_key, 6), dim), (parts,), jnp.float32, low / len(shards), largest / len(shards))
        gain = gain * jnp.repeat(jnp.exp(steps), extent[dim] // parts).reshape((-1,) + (1,) * (len(extent) - 1 - dim))
    return gain


def deal_out(stream_key, own, number, rows, number_of, top, most, skew):
    sequence = jax.random.permutation(stream_key, number_of)
    packed, usual = portions_of(number_of, rows * top, most, skew, True), portions_of(number_of, rows * top, most, skew, False)
    places = jnp.arange(number_of)

    def named(lengths, offset_by):
        used = int((lengths > 0).sum())
        fixed = max(1, used // 4)
        moved = fixed + (places - fixed + offset_by * (used - fixed)) % max(1, number_of - fixed)
        return jnp.zeros((number_of,), jnp.int32).at[sequence[jnp.where(places < fixed, places, moved)]].set(jnp.asarray(lengths, jnp.int32))

    lengths = jnp.where(number % 4 == 0, named(packed, number // 4), named(usual, number - number // 4 - 1))
    mixed = jax.random.permutation(jax.random.fold_in(own, 3), number_of)
    giver, taker = mixed[0:number_of // 2 * 2:2], mixed[1:number_of // 2 * 2:2]
    margin = jnp.minimum(lengths[giver] - 1, most - lengths[taker]) // 2
    margin = jnp.where((giver == sequence[0]) | (taker == sequence[0]) | (lengths[taker] == 0), 0, jnp.maximum(margin, 0))
    moved = jax.random.randint(jax.random.fold_in(own, 4), (number_of // 2,), 0, 1 << 20) % (margin + 1)
    lengths = lengths.at[giver].add(-moved).at[taker].add(moved)
    members = jnp.searchsorted(jnp.cumsum(lengths), jnp.arange(rows * top), side="right").astype(jnp.int32)
    listing = members.reshape(top, rows).T
    listing = listing[jax.random.permutation(jax.random.fold_in(own, 1), rows)]
    offset_by = jax.random.randint(jax.random.fold_in(own, 2), (rows, 1), 0, top)
    return jnp.take_along_axis(listing, (jnp.arange(top)[None, :] + offset_by) % top, axis=1)


def portions_of(number_of, total, most, lean, full):
    loads = [(1 << 20) // math.isqrt(standing ** lean) + 1 for standing in range(1, number_of + 1)]
    largest = most if full else min(most, max(-(-total // number_of), total * loads[0] // sum(loads)))
    least = 1 if total - largest >= number_of - 1 else 0
    given, rest = [largest] + [least] * (number_of - 1), total - largest - least * (number_of - 1)
    while rest > 0:
        free = [i for i in range(1, number_of) if given[i] < largest] or [i for i in range(1, number_of) if given[i] < most]
        whole, budget = sum([loads[i] for i in free]), rest
        for i in free:
            addition = min(most - given[i], max(1, budget * loads[i] // whole), rest)
            given[i] = given[i] + addition
            rest = rest - addition
    return np.array(given)


def centred(stream_key, dims, width, reach, pieces=(), kind=jnp.bfloat16):
    entries = jax.random.normal(stream_key, dims, jnp.float32) * width
    if len(pieces) > 0:
        entries = steps_of(stream_key, dims, pieces, -0.22, 0.18) * entries
    return jnp.clip(entries, min=-reach, max=reach).astype(kind)


def setup_inputs(seed: int = 0) -> dict:
    keys = jax.random.split(jax.random.key(seed), 8)
    tokens = centred(keys[0], (TOKENS, D), 1.0, 6.0, ((0, 64), (1, 2)))
    route_ids_keys = jax.random.split(jax.random.fold_in(keys[1], 1), TOKENS // TOK_DEV)
    route_ids_turns = jax.random.permutation(jax.random.fold_in(keys[1], 3), TOKENS // TOK_DEV)
    route_ids = jax.vmap(lambda own, number: deal_out(jax.random.fold_in(keys[1], 2), own, number, TOK_DEV, EXPERTS, TOP, CAP, 2))(route_ids_keys, route_ids_turns).reshape((TOKENS, TOP))
    route_weight = jnp.clip(jnp.exp(math.log(0.5) - 2.3025851 * jax.random.uniform(keys[2], (TOKENS, TOP), jnp.float32) ** steps_of(keys[2], (TOKENS, TOP), ((0, 64),), -0.2, 0.2)), 0.05, 0.5)
    gate_weight = centred(keys[3], (EXPERTS, FF, D), D ** -0.5, 0.09375, ((0, 64), (1, 2)))
    up_weight = centred(keys[4], (EXPERTS, FF, D), D ** -0.5, 0.09375, ((0, 64), (1, 2)))
    down_weight = centred(keys[5], (EXPERTS, FF, D), FF ** -0.5, 0.21875, ((0, 64), (1, 2)))
    out_grad = centred(keys[6], (TOKENS, D), 1.0, 6.0, ((0, 64), (1, 2)))
    return {"tokens": tokens, "route_ids": route_ids, "route_weight": route_weight, "gate_weight": gate_weight, "up_weight": up_weight, "down_weight": down_weight, "out_grad": out_grad}


def round_keep(value):
    return lax.optimization_barrier(value.astype(jnp.bfloat16)).astype(jnp.float32)


def one_expert(inputs):
    token_rows, slot_rows, gate_mat, up_mat, down_mat = inputs
    gate_act = jnp.dot(token_rows, gate_mat.T, preferred_element_type=jnp.float32)
    up_act = jnp.dot(token_rows, up_mat.T, preferred_element_type=jnp.float32)
    sigmoid_gate = jax.nn.sigmoid(gate_act)
    swish = gate_act * sigmoid_gate
    hidden = (swish * up_act).astype(jnp.bfloat16)
    hidden_grad = jnp.dot(slot_rows, down_mat.T, preferred_element_type=jnp.float32)
    gate_delta = (hidden_grad * up_act * sigmoid_gate * (1.0 + gate_act * (1.0 - sigmoid_gate))).astype(jnp.bfloat16)
    up_delta = (hidden_grad * swish).astype(jnp.bfloat16)
    group_width = FF // N_TENSOR
    out_sum = jnp.zeros((SLOTS, D), jnp.float32)
    back_sum = jnp.zeros((SLOTS, D), jnp.float32)
    for group in range(N_TENSOR):
        low = group * group_width
        high = low + group_width
        out_sum = out_sum + round_keep(jnp.dot(hidden[:, low:high], down_mat[low:high], preferred_element_type=jnp.float32))
        both_terms = jnp.dot(gate_delta[:, low:high], gate_mat[low:high], preferred_element_type=jnp.float32)
        both_terms = both_terms + jnp.dot(up_delta[:, low:high], up_mat[low:high], preferred_element_type=jnp.float32)
        back_sum = back_sum + round_keep(both_terms)
    gate_grad = jnp.dot(gate_delta.T, token_rows, preferred_element_type=jnp.float32).astype(jnp.bfloat16)
    up_grad = jnp.dot(up_delta.T, token_rows, preferred_element_type=jnp.float32).astype(jnp.bfloat16)
    down_grad = jnp.dot(hidden.T, slot_rows, preferred_element_type=jnp.float32).astype(jnp.bfloat16)
    return out_sum.astype(jnp.bfloat16), back_sum.astype(jnp.bfloat16), gate_grad, up_grad, down_grad


def reference(tokens, route_ids, route_weight, gate_weight, up_weight, down_weight, out_grad):
    per_block = TOK_DEV * TOP
    flat_ids = route_ids.reshape(-1).astype(jnp.int32)
    expert_hits = (flat_ids.reshape(N_EXPERT, per_block)[:, :, None] == jnp.arange(EXPERTS, dtype=jnp.int32)[None, None, :]).astype(jnp.int32)
    position = jnp.sum((jnp.cumsum(expert_hits, axis=1) - 1) * expert_hits, axis=2).reshape(-1).astype(jnp.int32)
    block_index = jnp.arange(TOKENS * TOP, dtype=jnp.int32) // per_block
    flat_slot = (flat_ids * SLOTS + block_index * CAP + position).astype(jnp.int32)
    repeated = jnp.repeat(tokens, TOP, axis=0)
    expert_rows = jnp.zeros((EXPERTS * SLOTS, D), tokens.dtype).at[flat_slot].set(repeated).reshape(EXPERTS, SLOTS, D)
    weighted = route_weight.reshape(-1)[:, None] * jnp.repeat(out_grad, TOP, axis=0).astype(jnp.float32)
    slot_grads = jnp.zeros((EXPERTS * SLOTS, D), tokens.dtype).at[flat_slot].set(weighted.astype(jnp.bfloat16)).reshape(EXPERTS, SLOTS, D)
    expert_out, expert_back, gate_grad, up_grad, down_grad = lax.map(one_expert, (expert_rows, slot_grads, gate_weight, up_weight, down_weight))
    picked = expert_out.reshape(EXPERTS * SLOTS, D)[flat_slot].astype(jnp.float32).reshape(TOKENS, TOP, D)
    mixed = jnp.sum(route_weight[:, :, None] * picked, axis=1).astype(jnp.bfloat16)
    route_grad = jnp.sum(picked * out_grad.astype(jnp.float32)[:, None, :], axis=2)
    returned = expert_back.reshape(EXPERTS * SLOTS, D)[flat_slot].astype(jnp.float32).reshape(TOKENS, TOP, D)
    tokens_grad = jnp.sum(returned, axis=1).astype(jnp.bfloat16)
    return mixed, tokens_grad, route_grad, gate_grad, up_grad, down_grad
```

```python
import jax
import jax.numpy as jnp
from jax import lax
from jax.experimental import pallas as pl
from jax.experimental.pallas import tpu as pltpu
from jax.sharding import PartitionSpec as P

MESH = pl.DeviceIdType.MESH
BF = jnp.bfloat16
F32 = jnp.float32
ROUTES = ((0, 1, 2), (2, 0, 1), (1, 2, 0))
STRIDE = (16, 4, 1)
WIDE = (768, 768, 512)
FROM = (0, 768, 1536)
HALF = 2048
HID = 384
PARTS = range(3)


def nt(left, right):
    return lax.dot_general(left, right, (((1,), (1,)), ((), ())), preferred_element_type=F32)


def tn(left, right):
    return lax.dot_general(left, right, (((0,), (0,)), ((), ())), preferred_element_type=F32)


def nn(left, right):
    return jnp.dot(left, right, preferred_element_type=F32)


class Copies:
    def __init__(self, send_sems, recv_sems):
        self.send_sems, self.recv_sems, self.used, self.open = send_sems, recv_sems, 0, []

    def start(self, src, dst, device):
        copy = pltpu.make_async_remote_copy(
            src_ref=src,
            dst_ref=dst,
            send_sem=self.send_sems.at[self.used],
            recv_sem=self.recv_sems.at[self.used],
            device_id=device,
            device_id_type=MESH,
        )
        self.used += 1
        copy.start()
        self.open.append(copy)
        return copy

    def sent(self, copies):
        for copy in copies:
            copy.wait_send()
            self.open = [other for other in self.open if other is not copy]

    def finish(self):
        self.sent(list(self.open))


def main_kernel(*refs):
    refs = list(refs)

    def take(n):
        got = refs[:n]
        del refs[:n]
        return got

    tok, og, tab, gw, uw, dw = take(6)
    mixed, tgrad, rgo, t_out, g_out, h_out, gd_out, ud_out = take(8)
    ag = [take(3), take(3)]
    send = [take(3), take(3)]
    own = [take(3), take(3)]
    oth = [take(3), take(3)]
    tabs = take(3)
    pick = take(3)
    pickw = take(3)
    wcol = take(3)
    both = [take(3) for _ in range(3)]
    rest = [take(3) for _ in range(3)]
    part = take(3)
    gact, uact, fa, fb = take(4)
    hid = take(3)
    gdel = take(3)
    udel = take(3)
    qbuf, qsib, qrec, rgsend, rg2, rg1send, rg1 = take(7)
    crecv = [take(3), take(3)]
    prec = [take(3), take(3)]
    p1send = [take(3), take(3)]
    p1rec = [take(3), take(3)]
    send_sems, recv_sems, wsems, osems = take(4)

    me = lax.axis_index("expert")
    t = lax.axis_index("tensor")
    c = (me // 16, (me // 4) % 4, me % 4)
    remote = Copies(send_sems, recv_sems)
    sib = (me, 1 - t)

    def at(dim, j):
        return lax.rem(c[dim] + j, 4)

    def peer(dim, j):
        return (me + (at(dim, j) - c[dim]) * STRIDE[dim], t)

    def rows(i, n):
        return pl.ds(pl.multiple_of(i * n, n), n)

    loads = []
    for w, src in enumerate((gw, uw, dw)):
        for k in PARTS:
            mine = pl.ds(pl.multiple_of(t * HALF + FROM[k], 128), WIDE[k])
            other = pl.ds(pl.multiple_of((1 - t) * HALF + FROM[k], 128), WIDE[k])
            loads.append(pltpu.make_async_copy(src.at[0, :, mine], both[w][k].at[pl.ds(0, HID)], wsems.at[w * 6 + k * 2]))
            loads.append(pltpu.make_async_copy(src.at[0, :, other], rest[w][k], wsems.at[w * 6 + k * 2 + 1]))
    for load in loads:
        load.start()

    barrier = pltpu.get_barrier_semaphore()
    for dim in PARTS:
        for j in (1, 2, 3):
            pl.semaphore_signal(barrier, inc=1, device_id=peer(dim, j), device_id_type=MESH)
    pl.semaphore_signal(barrier, inc=1, device_id=sib, device_id_type=MESH)
    pl.semaphore_wait(barrier, 10)

    first = [[], []]
    first_tab = []
    for k in PARTS:
        d1, d2, _ = ROUTES[k]
        first_tab.append([remote.start(tab, tabs[k].at[c[d2], c[d1]], peer(d1, j)) for j in (2, 1, 3)])
    for s, src in enumerate((tok, og)):
        for k in PARTS:
            d1, d2, _ = ROUTES[k]
            cols = pl.ds(FROM[k], WIDE[k])
            here = rows(c[d2] * 4 + c[d1], 32)
            first[s].append([remote.start(src.at[:, cols], ag[s][k].at[here], peer(d1, j)) for j in (2, 1, 3)])
    for k in PARTS:
        d1, d2, _ = ROUTES[k]
        tabs[k][c[d2], c[d1]] = tab[...]
        for s, src in enumerate((tok, og)):
            ag[s][k][rows(c[d2] * 4 + c[d1], 32), :] = src[:, pl.ds(FROM[k], WIDE[k])]

    def second(s, k):
        for copy in first[s][k]:
            copy.wait_recv()
        d2 = ROUTES[k][1]
        block = ag[s][k].at[rows(c[d2], 128)]
        return [remote.start(block, block, peer(d2, j)) for j in (2, 1, 3)]

    second_tab, second_tok = [], []
    for k in PARTS:
        for copy in first_tab[k]:
            copy.wait_recv()
        d2 = ROUTES[k][1]
        second_tab.append([remote.start(tabs[k].at[c[d2]], tabs[k].at[c[d2]], peer(d2, j)) for j in (2, 1, 3)])
    for k in PARTS:
        second_tok.append(second(0, k))

    swaps = [[None] * 3 for _ in range(3)]
    for i, load in enumerate(loads):
        load.wait()
    for w in range(3):
        for k in PARTS:
            swaps[w][k] = remote.start(rest[w][k], both[w][k].at[pl.ds(HID, HID)], sib)

    lane = lax.broadcasted_iota(jnp.int32, (16, 128), 1) // 32
    tri_r = lax.broadcasted_iota(jnp.int32, (128, 128), 0)
    tri_c = lax.broadcasted_iota(jnp.int32, (128, 128), 1)
    before = jnp.where((tri_r // 32 == tri_c // 32) & (tri_r < tri_c), 1.0, 0.0).astype(BF)
    slot_row = lax.broadcasted_iota(jnp.int32, (128, 512), 0).astype(F32)
    block_base = (lax.broadcasted_iota(jnp.int32, (8, 512), 1) // 32 * 8).astype(F32)
    sub = lax.broadcasted_iota(jnp.int32, (8, 512), 0)
    table_ids = []
    for k in PARTS:
        d3 = ROUTES[k][2]
        for copy in second_tab[k]:
            copy.wait_recv()
        tiles = []
        for c2 in range(4):
            tile = tabs[k][c2, 0]
            for c1 in range(1, 4):
                tile = jnp.where(lane == c1, tabs[k][c2, c1], tile)
            tiles.append(tile)
        tile = jnp.concatenate(tiles, axis=1)
        ids, wts = tile[:8], tile[8:]
        if k == 0:
            table_ids = (ids, wts)
        hits = jnp.zeros((8, 512), F32)
        wds = []
        for d in range(4):
            expert = (me + (d - c[d3]) * STRIDE[d3]).astype(F32)
            same = ids == expert
            hits = jnp.where(sub == d, jnp.sum(jnp.where(same, 1.0, 0.0), axis=0, keepdims=True), hits)
            wds.append(jnp.sum(jnp.where(same, wts, 0.0), axis=0, keepdims=True))
        place = jnp.concatenate([nn(hits[:, i * 128 : i * 128 + 128].astype(BF), before) for i in range(4)], axis=1)
        key = jnp.where(hits > 0.0, place + block_base, -1.0)
        for d in range(4):
            hit = key[d : d + 1, :] == slot_row
            weight = jnp.where(hit, wds[d], 0.0)
            pick[k][pl.ds(d * 128, 128), :] = jnp.where(hit, 1.0, 0.0).astype(BF)
            pickw[k][pl.ds(d * 128, 128), :] = weight.astype(BF)
            wcol[k][pl.ds(d * 128, 128), :] = jnp.sum(weight, axis=1, keepdims=True)

    def third(s, k, copies):
        d3 = ROUTES[k][2]
        for copy in copies:
            copy.wait_recv()
        out = []
        for j in (2, 1, 3, 0):
            d = rows(at(d3, j), 128)
            got = nn(pick[k][d, :], ag[s][k][...])
            if s == 1:
                got = got * wcol[k][d, :]
            if j == 0:
                own[s][k][rows(c[d3], 128), :] = got.astype(BF)
            else:
                send[s][k][d, :] = got.astype(BF)
                out.append(remote.start(send[s][k].at[d], own[s][k].at[rows(c[d3], 128)], peer(d3, j)))
        return out

    def forward(s, k, copies):
        d3 = ROUTES[k][2]
        out = []
        for j, copy in zip((0, 1, 3, 2), (None, copies[1], copies[2], copies[0])):
            if copy is not None:
                copy.wait_recv()
            r = rows(at(d3, 4 - j), 128)
            out.append(remote.start(own[s][k].at[r], oth[s][k].at[r], sib))
        return out

    third_tok = [third(0, k, second_tok[k]) for k in PARTS]
    second_og = [second(1, k) for k in PARTS]
    cross_tok = [forward(0, k, third_tok[k]) for k in PARTS]
    third_og = [third(1, k, second_og[k]) for k in PARTS]

    keep = []

    def store(src, dst):
        copy = pltpu.make_async_copy(src, dst, osems.at[len(keep)])
        copy.start()
        keep.append(copy)

    def keep_rows(s, k, dst):
        mine = pl.ds(pl.multiple_of(t * HALF + FROM[k], 128), WIDE[k])
        other = pl.ds(pl.multiple_of((1 - t) * HALF + FROM[k], 128), WIDE[k])
        store(own[s][k], dst.at[:, mine])
        store(oth[s][k], dst.at[:, other])

    def spot(k, x, y, z):
        v = (z, y, x)
        d1, d2, d3 = ROUTES[k]
        return pl.ds(pl.multiple_of(((v[d3] * 4 + v[d2]) * 4 + v[d1]) * 8, 8), 8)

    def contract(s, w, k):
        part[k][...] = nt(own[s][k][...], both[w][k][pl.ds(0, HID), :]) + nt(oth[s][k][...], rest[w][k][...])

    def gather_parts(dst):
        def body(i, carry):
            y, z = i // 4, i % 4
            for x in range(4):
                dst[spot(0, x, y, z), :] = (
                    part[0][spot(0, x, y, z), :] + part[1][spot(1, x, y, z), :] + part[2][spot(2, x, y, z), :]
                )
            return carry

        lax.fori_loop(0, 16, body, 0)

    def spread(src, dst):
        dst[0][:, pl.ds(0, HID)] = src[...].astype(BF)

        def body(i, carry):
            a, b = i // 4, i % 4
            group = rows(i, 32)
            dst[1][group, pl.ds(0, HID)] = jnp.concatenate([src[spot(0, x, a, b), :] for x in range(4)], axis=0).astype(BF)
            dst[2][group, pl.ds(0, HID)] = jnp.concatenate([src[spot(0, b, y, a), :] for y in range(4)], axis=0).astype(BF)
            return carry

        lax.fori_loop(0, 16, body, 0)

    def swap_cols(dst):
        return [remote.start(dst[k].at[:, pl.ds(0, HID)], dst[k].at[:, pl.ds(HID, HID)], sib) for k in PARTS]

    for k in PARTS:
        for copy in cross_tok[k]:
            copy.wait_recv()
        keep_rows(0, k, t_out)
    for k in PARTS:
        contract(0, 0, k)
    gather_parts(gact)
    for k in PARTS:
        contract(0, 1, k)
    gather_parts(uact)
    gate = gact[...]
    fa[...] = gate * jax.nn.sigmoid(gate) * uact[...]
    spread(fa, hid)
    cross_hid = swap_cols(hid)
    for k in PARTS:
        store(hid[k].at[:, pl.ds(0, HID)], h_out.at[k])

    cross_og = [forward(1, k, third_og[k]) for k in PARTS]

    def back3(s, k):
        d3 = ROUTES[k][2]
        out = []
        for j in (2, 1, 3):
            out.append(remote.start(send[s][k].at[rows(at(d3, j), 128)], crecv[s][k].at[rows(c[d3], 128)], peer(d3, j)))
        crecv[s][k][rows(c[d3], 128), :] = send[s][k][rows(c[d3], 128), :]
        return out

    def back2(s, k, copies):
        for copy in copies:
            copy.wait_recv()
        ag[s][k][...] = tn((pickw, pick)[s][k][...], crecv[s][k][...]).astype(BF)
        d2 = ROUTES[k][1]
        return [remote.start(ag[s][k].at[rows(at(d2, j), 128)], prec[s][k].at[j - 1], peer(d2, j)) for j in (2, 1, 3)]

    def back1(s, k, copies):
        for copy in copies:
            copy.wait_recv()
        d1, d2, _ = ROUTES[k]
        total = ag[s][k][rows(c[d2], 128), :].astype(F32)
        for j in range(3):
            total = total + prec[s][k][j].astype(F32)
        p1send[s][k][...] = total.astype(BF)
        return [remote.start(p1send[s][k].at[rows(at(d1, j), 32)], p1rec[s][k].at[j - 1], peer(d1, j)) for j in (2, 1, 3)]

    def back0(s, k, copies, dst):
        for copy in copies:
            copy.wait_recv()
        total = p1send[s][k][rows(c[ROUTES[k][0]], 32), :].astype(F32)
        for j in range(3):
            total = total + p1rec[s][k][j].astype(F32)
        dst[:, pl.ds(FROM[k], WIDE[k])] = total.astype(BF)

    out3 = []
    for k in PARTS:
        swaps[2][k].wait_recv()
        cross_hid[k].wait_recv()
        remote.sent(second_tok[k])
        remote.sent(third_tok[k])
        send[0][k][...] = nn(hid[k][...], both[2][k][...]).astype(BF)
        out3.append(back3(0, k))

    for k in PARTS:
        for copy in cross_og[k]:
            copy.wait_recv()
        keep_rows(1, k, g_out)
    for k in PARTS:
        contract(1, 2, k)
    gather_parts(fb)
    qprod = fa[...].astype(BF).astype(F32) * fb[...]
    qbuf[...] = lax.dot_general(
        jnp.ones((8, HID), F32), qprod, (((1,), (1,)), ((), ())), precision=lax.Precision.HIGHEST, preferred_element_type=F32
    )
    cross_q = remote.start(qbuf, qsib, sib)
    gate = gact[...]
    sg = jax.nn.sigmoid(gate)
    fa[...] = fb[...] * uact[...] * sg * (1.0 + gate * (1.0 - sg))
    spread(fa, gdel)
    cross_gd = swap_cols(gdel)
    fa[...] = fb[...] * (gate * sg)
    spread(fa, udel)
    cross_ud = swap_cols(udel)
    for k in PARTS:
        store(gdel[k].at[:, pl.ds(0, HID)], gd_out.at[k])
        store(udel[k].at[:, pl.ds(0, HID)], ud_out.at[k])

    out2 = [back2(0, k, out3[k]) for k in PARTS]

    d1, d2, d3 = ROUTES[0]
    cross_q.wait_recv()
    q = qbuf[...] + qsib[...]
    for i in range(4):
        rgsend[i] = q[:, i * 128 : i * 128 + 128]
    rg3 = [remote.start(rgsend.at[at(d3, j)], qrec.at[c[d3]], peer(d3, j)) for j in (2, 1, 3)]
    qrec[c[d3]] = rgsend[c[d3]]

    bk3 = []
    for k in PARTS:
        for w in range(2):
            swaps[w][k].wait_recv()
        cross_gd[k].wait_recv()
        cross_ud[k].wait_recv()
        remote.sent(second_og[k])
        remote.sent(third_og[k])
        send[1][k][...] = (nn(gdel[k][...], both[0][k][...]) + nn(udel[k][...], both[1][k][...])).astype(BF)
        bk3.append(back3(1, k))

    for copy in rg3:
        copy.wait_recv()
    ids, wts = table_ids
    rg = jnp.zeros((8, 512), F32)
    for d in range(4):
        value = jnp.dot(
            qrec[d],
            pick[0][pl.ds(d * 128, 128), :].astype(F32),
            precision=lax.Precision.HIGHEST,
            preferred_element_type=F32,
        )
        expert = (me + (d - c[d3]) * STRIDE[d3]).astype(F32)
        rg = rg + jnp.where(ids == expert, value, 0.0)
    rg = rg / wts
    remote.sent(rg3)
    for i in range(4):
        rgsend[i] = rg[:, i * 128 : i * 128 + 128]
    rgc2 = [remote.start(rgsend.at[at(d2, j)], rg2.at[j - 1], peer(d2, j)) for j in (2, 1, 3)]

    out1 = [back1(0, k, out2[k]) for k in PARTS]
    for copy in rgc2:
        copy.wait_recv()
    rg1send[...] = rgsend[c[d2]] + rg2[0] + rg2[1] + rg2[2]
    rgc1 = [remote.start(rg1send, rg1.at[j - 1], peer(d1, j)) for j in (2, 1, 3)]
    bk2 = [back2(1, k, bk3[k]) for k in PARTS]
    for k in PARTS:
        back0(0, k, out1[k], mixed)
    for copy in rgc1:
        copy.wait_recv()
    rgo[...] = rg1send[...] + rg1[0] + rg1[1] + rg1[2]
    bk1 = [back1(1, k, bk2[k]) for k in PARTS]
    for copy in keep:
        copy.wait()
    for k in PARTS:
        back0(1, k, bk1[k], tgrad)
    remote.finish()


N_COPIES = 220


def run_main(tok, og, tab, gw, uw, dw):
    vm = pltpu.VMEM
    scratch = []

    def per(make):
        scratch.extend(make(WIDE[k]) for k in PARTS)

    for _ in range(8):
        per(lambda w: vm((512, w), BF))
    per(lambda w: vm((4, 4, 16, 128), F32))
    per(lambda w: vm((512, 512), BF))
    per(lambda w: vm((512, 512), BF))
    per(lambda w: vm((512, 1), F32))
    for _ in range(3):
        per(lambda w: vm((2 * HID, w), BF))
    for _ in range(3):
        per(lambda w: vm((HID, w), BF))
    per(lambda w: vm((512, HID), F32))
    scratch.extend(vm((512, HID), F32) for _ in range(4))
    for _ in range(3):
        per(lambda w: vm((512, 2 * HID), BF))
    scratch.extend(vm(s, F32) for s in ((8, 512), (8, 512), (4, 8, 128), (4, 8, 128), (3, 8, 128), (8, 128), (3, 8, 128)))
    for _ in range(2):
        per(lambda w: vm((512, w), BF))
    for _ in range(2):
        per(lambda w: vm((3, 128, w), BF))
    for _ in range(2):
        per(lambda w: vm((128, w), BF))
    for _ in range(2):
        per(lambda w: vm((3, 32, w), BF))
    scratch.extend(
        [
            pltpu.SemaphoreType.DMA((N_COPIES,)),
            pltpu.SemaphoreType.DMA((N_COPIES,)),
            pltpu.SemaphoreType.DMA((18,)),
            pltpu.SemaphoreType.DMA((24,)),
        ]
    )
    in_vmem = pl.BlockSpec(memory_space=pltpu.VMEM)
    anywhere = pl.BlockSpec(memory_space=pl.ANY)
    shape = jax.ShapeDtypeStruct
    return pl.pallas_call(
        main_kernel,
        out_shape=(
            shape((32, HALF), BF),
            shape((32, HALF), BF),
            shape((8, 128), F32),
            shape((512, 2 * HALF), BF),
            shape((512, 2 * HALF), BF),
            shape((3, 512, HID), BF),
            shape((3, 512, HID), BF),
            shape((3, 512, HID), BF),
        ),
        in_specs=[in_vmem] * 3 + [anywhere] * 3,
        out_specs=(in_vmem,) * 3 + (anywhere,) * 5,
        scratch_shapes=scratch,
        compiler_params=pltpu.CompilerParams(collective_id=0, has_side_effects=True, vmem_limit_bytes=63 * 2**20),
        cost_estimate=pl.CostEstimate(flops=10**10, bytes_accessed=2 * 10**7, transcendentals=10**6),
    )(tok, og, tab, gw, uw, dw)


def grads_kernel(t_ref, g_ref, h_ref, gd_ref, ud_ref, gg_ref, ug_ref, dg_ref):
    gg_ref[0] = tn(gd_ref[0], t_ref[...]).astype(BF)
    ug_ref[0] = tn(ud_ref[0], t_ref[...]).astype(BF)
    dg_ref[0] = tn(h_ref[0], g_ref[...]).astype(BF)


def run_grads(t_rows, g_rows, h, gd, ud):
    tile = 256
    cols = pl.BlockSpec((512, tile), lambda i: (0, i))
    left = pl.BlockSpec((1, 512, HID), lambda i: (i % 8 // 3, 0, 0))
    out = pl.BlockSpec((1, HID, tile), lambda i: (0, 0, i))
    return pl.pallas_call(
        grads_kernel,
        grid=(2 * HALF // tile,),
        out_shape=(jax.ShapeDtypeStruct((1, HID, 2 * HALF), BF),) * 3,
        in_specs=[cols, cols, left, left, left],
        out_specs=(out,) * 3,
        compiler_params=pltpu.CompilerParams(vmem_limit_bytes=48 * 2**20),
        cost_estimate=pl.CostEstimate(flops=5 * 10**9, bytes_accessed=2 * 10**7, transcendentals=0),
    )(t_rows, g_rows, h, gd, ud)


def shards(tokens, route_ids, route_weight, gate_weight, up_weight, down_weight, out_grad):
    tab = jnp.concatenate(
        [jnp.tile(route_ids.astype(F32).T, (1, 4)), jnp.tile(route_weight.T, (1, 4))], axis=0
    )
    mixed, tgrad, rg, t_rows, g_rows, h, gd, ud = run_main(
        tokens, out_grad, tab, gate_weight, up_weight, down_weight
    )
    gate_grad, up_grad, down_grad = run_grads(t_rows, g_rows, h, gd, ud)
    z = lax.axis_index("expert") // 16
    route_grad = lax.dynamic_slice_in_dim(rg, z * 32, 32, axis=1).T
    return (mixed, tgrad, route_grad, gate_grad, up_grad, down_grad)


def solution(mesh):
    placed = (
        P("expert", "tensor"),
        P("expert", None),
        P("expert", None),
        P("expert", "tensor", None),
        P("expert", "tensor", None),
        P("expert", "tensor", None),
        P("expert", "tensor"),
    )
    return jax.shard_map(
        shards,
        mesh=mesh,
        in_specs=placed,
        out_specs=(
            P("expert", "tensor"),
            P("expert", "tensor"),
            P("expert", None),
            P("expert", "tensor", None),
            P("expert", "tensor", None),
            P("expert", "tensor", None),
        ),
        check_vma=False,
    )
```

```python
import jax
import jax.numpy as jnp
from jax import lax
from jax.experimental import pallas as pl
from jax.experimental.pallas import tpu as pltpu
from jax.sharding import PartitionSpec as P

MESH = pl.DeviceIdType.MESH
BF = jnp.bfloat16
F32 = jnp.float32
ROUTES = ((0, 1, 2), (2, 0, 1), (1, 2, 0))
STRIDE = (16, 4, 1)
WIDE = (768, 768, 512)
FROM = (0, 768, 1536)
HALF = 2048
HID = 384
PARTS = range(3)


def nt(left, right):
    return lax.dot_general(left, right, (((1,), (1,)), ((), ())), preferred_element_type=F32)


def tn(left, right):
    return lax.dot_general(left, right, (((0,), (0,)), ((), ())), preferred_element_type=F32)


def nn(left, right):
    return jnp.dot(left, right, preferred_element_type=F32)


class Group:
    def __init__(self, index, send_sem, recv_sem, whole, device):
        self.index, self.send_sem, self.recv_sem, self.open = index, send_sem, recv_sem, True
        self.all = pltpu.make_async_remote_copy(
            src_ref=whole, dst_ref=whole, send_sem=send_sem, recv_sem=recv_sem, device_id=device, device_id_type=MESH
        )

    def start(self, src, dst, device):
        pltpu.make_async_remote_copy(
            src_ref=src, dst_ref=dst, send_sem=self.send_sem, recv_sem=self.recv_sem, device_id=device, device_id_type=MESH
        ).start()

    def arrived(self):
        self.all.wait_recv()

    def sent(self):
        if self.open:
            self.all.wait_send()
        self.open = False


class Copies:
    def __init__(self, send_sems, recv_sems, device):
        self.send_sems, self.recv_sems, self.device, self.groups = send_sems, recv_sems, device, []

    def group(self, whole):
        i = len(self.groups)
        self.groups.append(Group(i, self.send_sems.at[i], self.recv_sems.at[i], whole, self.device))
        return self.groups[i]

    def one(self, src, dst, device):
        group = self.group(src)
        group.start(src, dst, device)
        return group

    def finish(self):
        for group in self.groups:
            group.sent()


def main_kernel(*refs):
    refs = list(refs)

    def take(n):
        got = refs[:n]
        del refs[:n]
        return got

    tok, og, ids_in, wts_in, gw, uw, dw = take(7)
    mixed, tgrad, rgo, t_out, g_out, h_out, gd_out, ud_out = take(8)
    (tab,) = take(1)
    ag = [take(3), take(3)]
    send = [take(3), take(3)]
    own = [take(3), take(3)]
    oth = [take(3), take(3)]
    tabs = take(3)
    pick = take(3)
    pickw = take(3)
    wcol = take(3)
    both = [take(3) for _ in range(3)]
    rest = [take(3) for _ in range(3)]
    part = take(3)
    gact, uact, fa, fb = take(4)
    hid = take(3)
    gdel = take(3)
    udel = take(3)
    qbuf, qsib, qrec, rgsend, rg2, rg1send, rg1 = take(7)
    crecv = [take(3), take(3)]
    prec = [take(3), take(3)]
    p1send = [take(3), take(3)]
    p1rec = [take(3), take(3)]
    send_sems, recv_sems, wsems, osems = take(4)

    me = lax.axis_index("expert")
    t = lax.axis_index("tensor")
    c = (me // 16, (me // 4) % 4, me % 4)
    sib = (me, 1 - t)
    remote = Copies(send_sems, recv_sems, sib)

    def at(dim, j):
        return lax.rem(c[dim] + j, 4)

    def peer(dim, j):
        return (me + (at(dim, j) - c[dim]) * STRIDE[dim], t)

    def rows(i, n):
        return pl.ds(pl.multiple_of(i * n, n), n)

    def expert_at(d3, d):
        return (me + (d - c[d3]) * STRIDE[d3]).astype(F32)

    barrier = pltpu.get_barrier_semaphore()
    for dim in PARTS:
        for j in (1, 2, 3):
            pl.semaphore_signal(barrier, inc=1, device_id=peer(dim, j), device_id_type=MESH)
    pl.semaphore_signal(barrier, inc=1, device_id=sib, device_id_type=MESH)

    loads = []
    for w, src in enumerate((gw, uw, dw)):
        for k in PARTS:
            mine = pl.ds(pl.multiple_of(t * HALF + FROM[k], 128), WIDE[k])
            other = pl.ds(pl.multiple_of((1 - t) * HALF + FROM[k], 128), WIDE[k])
            pltpu.make_async_copy(src.at[0, :, other], rest[w][k], wsems.at[w]).start()
            pltpu.make_async_copy(src.at[0, :, mine], both[w][k].at[pl.ds(0, HID)], wsems.at[w]).start()
        loads.append(pltpu.make_async_copy(src, src, wsems.at[w]))

    tab[0:8, :] = jnp.concatenate([ids_in[...].astype(F32)] * 4, axis=1)
    tab[8:16, :] = jnp.concatenate([wts_in[...]] * 4, axis=1)
    for k in PARTS:
        d1, d2, _ = ROUTES[k]
        tabs[k][c[d2], c[d1]] = tab[...]
        for s, src in enumerate((tok, og)):
            ag[s][k][rows(c[d2] * 4 + c[d1], 32), :] = src[:, pl.ds(FROM[k], WIDE[k])]
    pl.semaphore_wait(barrier, 10)

    first = [[], []]
    first_tab = []
    for k in PARTS:
        d1, d2, _ = ROUTES[k]
        first_tab.append(remote.group(tabs[k].at[0, pl.ds(0, 3)]))
        for j in (2, 1, 3):
            first_tab[k].start(tab, tabs[k].at[c[d2], c[d1]], peer(d1, j))
    for s, src in enumerate((tok, og)):
        for k in PARTS:
            d1, d2, _ = ROUTES[k]
            cols = pl.ds(FROM[k], WIDE[k])
            here = rows(c[d2] * 4 + c[d1], 32)
            first[s].append(remote.group(ag[s][k].at[pl.ds(0, 96)]))
            for j in (2, 1, 3):
                first[s][k].start(src.at[:, cols], ag[s][k].at[here], peer(d1, j))

    def second(s, k):
        first[s][k].arrived()
        d2 = ROUTES[k][1]
        block = ag[s][k].at[rows(c[d2], 128)]
        return {j: remote.one(block, block, peer(d2, j)) for j in (2, 1, 3)}

    lane16 = lax.broadcasted_iota(jnp.int32, (16, 128), 1) // 32
    tri_r = lax.broadcasted_iota(jnp.int32, (128, 128), 0)
    tri_c = lax.broadcasted_iota(jnp.int32, (128, 128), 1)
    before = jnp.where((tri_r // 32 == tri_c // 32) & (tri_r < tri_c), 1.0, 0.0).astype(BF)
    slot_row = lax.broadcasted_iota(jnp.int32, (32, 128), 0).astype(F32)
    lane8 = lax.broadcasted_iota(jnp.int32, (8, 128), 1) // 32
    block_base = (lane8 * 8).astype(F32)
    sub8 = lax.broadcasted_iota(jnp.int32, (8, 128), 0)

    def table(k, c2):
        tile = tabs[k][c2, 0]
        for c1 in range(1, 4):
            tile = jnp.where(lane16 == c1, tabs[k][c2, c1], tile)
        return tile[:8], tile[8:]

    def tables(k, c2):
        d3 = ROUTES[k][2]
        ids, wts = table(k, c2)
        hits = jnp.zeros((8, 128), F32)
        wds = []
        for d in range(4):
            same = ids == expert_at(d3, d)
            hits = jnp.where(sub8 == d, jnp.sum(jnp.where(same, 1.0, 0.0), axis=0, keepdims=True), hits)
            wds.append(jnp.sum(jnp.where(same, wts, 0.0), axis=0, keepdims=True))
        key = jnp.where(hits > 0.0, nn(hits.astype(BF), before) + block_base, -1.0)
        hit = [key[d : d + 1, :] == slot_row for d in range(4)]
        weight = jnp.concatenate([jnp.where(hit[d], wds[d], 0.0) for d in range(4)], axis=0)
        group = rows(c2, 128)
        pick[k][group, :] = jnp.concatenate([jnp.where(h, 1.0, 0.0) for h in hit], axis=0).astype(BF)
        pickw[k][group, :] = weight.astype(BF)
        wcol[k][group, :] = jnp.sum(weight, axis=1, keepdims=True)

    def third(s, k, j):
        _, d2, d3 = ROUTES[k]
        c2 = at(d2, j)
        group = rows(c2, 128)
        got = nn(pick[k][group, :], ag[s][k][group, :])
        if s == 1:
            got = got * wcol[k][group, :]
        send[s][k][group, :] = got.astype(BF)
        here = rows(c[d3] * 4 + c2, 32)
        for j3 in (2, 1, 3):
            thirds[s][k][j3].start(send[s][k].at[rows(c2 * 4 + at(d3, j3), 32)], own[s][k].at[here], peer(d3, j3))
        own[s][k][here, :] = send[s][k][rows(c2 * 4 + c[d3], 32), :]

    def forward(s, k):
        d3 = ROUTES[k][2]
        out = remote.group(oth[s][k])
        for j3 in (0, 1, 3, 2):
            if j3:
                thirds[s][k][j3].arrived()
            r = rows(at(d3, 4 - j3), 128)
            out.start(own[s][k].at[r], oth[s][k].at[r], sib)
        return out

    thirds = [[{j3: remote.group(own[s][k].at[pl.ds(0, 128)]) for j3 in (1, 2, 3)} for k in PARTS] for s in range(2)]
    seconds, second_tab = [[], []], []
    for k in PARTS:
        first_tab[k].arrived()
        d2 = ROUTES[k][1]
        second_tab.append({j: remote.one(tabs[k].at[c[d2]], tabs[k].at[c[d2]], peer(d2, j)) for j in (2, 1, 3)})
    for k in PARTS:
        seconds[0].append(second(0, k))
    for k in PARTS:
        tables(k, c[ROUTES[k][1]])
        third(0, k, 0)
    for k in PARTS:
        seconds[1].append(second(1, k))
    for k in PARTS:
        third(1, k, 0)

    for load in loads:
        load.wait()
    swaps = [[remote.one(rest[w][k], both[w][k].at[pl.ds(HID, HID)], sib) for k in PARTS] for w in range(3)]

    for j in (1, 3, 2):
        for k in PARTS:
            second_tab[k][j].arrived()
            tables(k, at(ROUTES[k][1], 4 - j))
            seconds[0][k][j].arrived()
            third(0, k, 4 - j)
    for j in (1, 3, 2):
        for k in PARTS:
            seconds[1][k][j].arrived()
            third(1, k, 4 - j)

    def store(src, dst, i):
        pltpu.make_async_copy(src, dst, osems.at[i]).start()

    def keep_rows(s, k, dst):
        mine = pl.ds(pl.multiple_of(t * HALF + FROM[k], 128), WIDE[k])
        other = pl.ds(pl.multiple_of((1 - t) * HALF + FROM[k], 128), WIDE[k])
        store(own[s][k], dst.at[:, mine], s)
        store(oth[s][k], dst.at[:, other], s)

    def spot(k, x, y, z):
        v = (z, y, x)
        d1, d2, d3 = ROUTES[k]
        return pl.ds(pl.multiple_of(((v[d3] * 4 + v[d2]) * 4 + v[d1]) * 8, 8), 8)

    def contract(s, w, k):
        part[k][...] = nt(own[s][k][...], both[w][k][pl.ds(0, HID), :]) + nt(oth[s][k][...], rest[w][k][...])

    def gather_parts(dst):
        def body(i, carry):
            y, z = i // 4, i % 4
            for x in range(4):
                dst[spot(0, x, y, z), :] = (
                    part[0][spot(0, x, y, z), :] + part[1][spot(1, x, y, z), :] + part[2][spot(2, x, y, z), :]
                )
            return carry

        lax.fori_loop(0, 16, body, 0)

    def spread(src, dst):
        dst[0][:, pl.ds(0, HID)] = src[...].astype(BF)

        def body(i, carry):
            a, b = i // 4, i % 4
            group = rows(i, 32)
            dst[1][group, pl.ds(0, HID)] = jnp.concatenate([src[spot(0, x, a, b), :] for x in range(4)], axis=0).astype(BF)
            dst[2][group, pl.ds(0, HID)] = jnp.concatenate([src[spot(0, b, y, a), :] for y in range(4)], axis=0).astype(BF)
            return carry

        lax.fori_loop(0, 16, body, 0)

    def swap_cols(dst):
        return [remote.one(dst[k].at[:, pl.ds(0, HID)], dst[k].at[:, pl.ds(HID, HID)], sib) for k in PARTS]

    cross_tok = [forward(0, k) for k in PARTS]
    for k in PARTS:
        cross_tok[k].arrived()
        keep_rows(0, k, t_out)
        contract(0, 0, k)
    gather_parts(gact)
    for k in PARTS:
        contract(0, 1, k)
    gather_parts(uact)
    gate = gact[...]
    fa[...] = gate * jax.nn.sigmoid(gate) * uact[...]
    spread(fa, hid)
    cross_hid = swap_cols(hid)
    for k in PARTS:
        store(hid[k].at[:, pl.ds(0, HID)], h_out.at[k], 2)

    def reuse(s, k):
        for j in (1, 2, 3):
            seconds[s][k][j].sent()
            thirds[s][k][j].sent()

    def back3(s, k):
        _, d2, d3 = ROUTES[k]
        out = {}
        for j in (2, 1, 3, 0):
            c2 = at(d2, j)
            here = rows(c2 * 4 + c[d3], 32)
            out[j] = remote.group(crecv[s][k].at[pl.ds(0, 96)])
            for j3 in (2, 1, 3):
                out[j].start(send[s][k].at[rows(at(d3, j3) * 4 + c2, 32)], crecv[s][k].at[here], peer(d3, j3))
            crecv[s][k][here, :] = send[s][k][rows(c[d3] * 4 + c2, 32), :]
        return out

    def back2(s, k, thirds_back):
        d2 = ROUTES[k][1]
        out = remote.group(prec[s][k])
        for j in (2, 1, 3, 0):
            thirds_back[j].arrived()
            group = rows(at(d2, j), 128)
            ag[s][k][group, :] = tn((pickw, pick)[s][k][group, :], crecv[s][k][group, :]).astype(BF)
            if j:
                out.start(ag[s][k].at[group], prec[s][k].at[j - 1], peer(d2, j))
        return out

    def back1(s, k, seconds_back):
        seconds_back.arrived()
        d1, d2, _ = ROUTES[k]
        total = ag[s][k][rows(c[d2], 128), :].astype(F32)
        for j in range(3):
            total = total + prec[s][k][j].astype(F32)
        p1send[s][k][...] = total.astype(BF)
        out = remote.group(p1rec[s][k])
        for j in (2, 1, 3):
            out.start(p1send[s][k].at[rows(at(d1, j), 32)], p1rec[s][k].at[j - 1], peer(d1, j))
        return out

    def back0(s, k, firsts_back, dst):
        firsts_back.arrived()
        total = p1send[s][k][rows(c[ROUTES[k][0]], 32), :].astype(F32)
        for j in range(3):
            total = total + p1rec[s][k][j].astype(F32)
        dst[:, pl.ds(FROM[k], WIDE[k])] = total.astype(BF)

    out3 = []
    for k in PARTS:
        swaps[2][k].arrived()
        cross_hid[k].arrived()
        reuse(0, k)
        send[0][k][...] = nn(hid[k][...], both[2][k][...]).astype(BF)
        out3.append(back3(0, k))

    cross_og = [forward(1, k) for k in PARTS]
    for k in PARTS:
        cross_og[k].arrived()
        keep_rows(1, k, g_out)
        contract(1, 2, k)
    gather_parts(fb)
    gate = gact[...]
    sg = jax.nn.sigmoid(gate)
    qprod = fa[...].astype(BF).astype(F32) * fb[...]
    fa[...] = fb[...] * uact[...] * sg * (1.0 + gate * (1.0 - sg))
    spread(fa, gdel)
    cross_gd = swap_cols(gdel)
    fa[...] = fb[...] * (gate * sg)
    spread(fa, udel)
    cross_ud = swap_cols(udel)
    qbuf[...] = lax.dot_general(
        jnp.ones((8, HID), F32), qprod, (((1,), (1,)), ((), ())), precision=lax.Precision.HIGHEST, preferred_element_type=F32
    )
    cross_q = remote.one(qbuf, qsib, sib)
    for k in PARTS:
        store(gdel[k].at[:, pl.ds(0, HID)], gd_out.at[k], 3)
        store(udel[k].at[:, pl.ds(0, HID)], ud_out.at[k], 4)

    out2 = [back2(0, k, out3[k]) for k in PARTS]

    bk3 = []
    for k in PARTS:
        for w in range(2):
            swaps[w][k].arrived()
        cross_gd[k].arrived()
        cross_ud[k].arrived()
        reuse(1, k)
        send[1][k][...] = (nn(gdel[k][...], both[0][k][...]) + nn(udel[k][...], both[1][k][...])).astype(BF)
        bk3.append(back3(1, k))

    d1, d2, d3 = ROUTES[0]
    cross_q.arrived()
    q = qbuf[...] + qsib[...]
    for i in range(4):
        rgsend[i] = q[:, i * 128 : i * 128 + 128]
    rg3 = remote.group(qrec.at[pl.ds(0, 3)])
    for j in (2, 1, 3):
        rg3.start(rgsend.at[at(d3, j)], qrec.at[c[d3]], peer(d3, j))
    qrec[c[d3]] = rgsend[c[d3]]

    out1 = [back1(0, k, out2[k]) for k in PARTS]

    rg3.arrived()
    rg3.sent()
    for c2 in range(4):
        ids, wts = table(0, c2)
        spots = jnp.concatenate([qrec[d][:, c2 * 32 : c2 * 32 + 32] for d in range(4)], axis=1)
        values = jnp.dot(
            jnp.where(sub8 == lane8, spots, 0.0),
            pick[0][pl.ds(c2 * 128, 128), :].astype(F32),
            precision=lax.Precision.HIGHEST,
            preferred_element_type=F32,
        )
        rg = jnp.zeros((8, 128), F32)
        for d in range(4):
            rg = rg + jnp.where(ids == expert_at(d3, d), values[d : d + 1, :], 0.0)
        rgsend[c2] = rg / wts
    rgc2 = remote.group(rg2)
    for j in (2, 1, 3):
        rgc2.start(rgsend.at[at(d2, j)], rg2.at[j - 1], peer(d2, j))

    bk2 = [back2(1, k, bk3[k]) for k in PARTS]
    rgc2.arrived()
    rg1send[...] = rgsend[c[d2]] + rg2[0] + rg2[1] + rg2[2]
    rgc1 = remote.group(rg1)
    for j in (2, 1, 3):
        rgc1.start(rg1send, rg1.at[j - 1], peer(d1, j))
    for k in PARTS:
        back0(0, k, out1[k], mixed)
    rgc1.arrived()
    rg = rg1send[...] + rg1[0] + rg1[1] + rg1[2]
    mine = rg[:, 0:32]
    for i in range(1, 4):
        mine = jnp.where(c[d1] == i, rg[:, i * 32 : i * 32 + 32], mine)
    rgo[...] = mine
    bk1 = [back1(1, k, bk2[k]) for k in PARTS]
    for i, dst in enumerate((t_out, g_out, h_out, gd_out, ud_out)):
        pltpu.make_async_copy(dst, dst, osems.at[i]).wait()
    for k in PARTS:
        back0(1, k, bk1[k], tgrad)
    remote.finish()


N_GROUPS = 124


def run_main(tok, og, ids, wts, gw, uw, dw):
    vm = pltpu.VMEM
    scratch = [vm((16, 128), F32)]

    def per(make):
        scratch.extend(make(WIDE[k]) for k in PARTS)

    for _ in range(8):
        per(lambda w: vm((512, w), BF))
    per(lambda w: vm((4, 4, 16, 128), F32))
    per(lambda w: vm((512, 128), BF))
    per(lambda w: vm((512, 128), BF))
    per(lambda w: vm((512, 1), F32))
    for _ in range(3):
        per(lambda w: vm((2 * HID, w), BF))
    for _ in range(3):
        per(lambda w: vm((HID, w), BF))
    per(lambda w: vm((512, HID), F32))
    scratch.extend(vm((512, HID), F32) for _ in range(4))
    for _ in range(3):
        per(lambda w: vm((512, 2 * HID), BF))
    scratch.extend(vm(s, F32) for s in ((8, 512), (8, 512), (4, 8, 128), (4, 8, 128), (3, 8, 128), (8, 128), (3, 8, 128)))
    for _ in range(2):
        per(lambda w: vm((512, w), BF))
    for _ in range(2):
        per(lambda w: vm((3, 128, w), BF))
    for _ in range(2):
        per(lambda w: vm((128, w), BF))
    for _ in range(2):
        per(lambda w: vm((3, 32, w), BF))
    scratch.extend(
        [
            pltpu.SemaphoreType.DMA((N_GROUPS,)),
            pltpu.SemaphoreType.DMA((N_GROUPS,)),
            pltpu.SemaphoreType.DMA((3,)),
            pltpu.SemaphoreType.DMA((5,)),
        ]
    )
    in_vmem = pl.BlockSpec(memory_space=pltpu.VMEM)
    anywhere = pl.BlockSpec(memory_space=pl.ANY)
    shape = jax.ShapeDtypeStruct
    return pl.pallas_call(
        main_kernel,
        out_shape=(
            shape((32, HALF), BF),
            shape((32, HALF), BF),
            shape((8, 32), F32),
            shape((512, 2 * HALF), BF),
            shape((512, 2 * HALF), BF),
            shape((3, 512, HID), BF),
            shape((3, 512, HID), BF),
            shape((3, 512, HID), BF),
        ),
        in_specs=[in_vmem] * 4 + [anywhere] * 3,
        out_specs=(in_vmem,) * 3 + (anywhere,) * 5,
        scratch_shapes=scratch,
        compiler_params=pltpu.CompilerParams(collective_id=0, has_side_effects=True, vmem_limit_bytes=63 * 2**20),
        cost_estimate=pl.CostEstimate(flops=10**10, bytes_accessed=2 * 10**7, transcendentals=10**6),
    )(tok, og, ids, wts, gw, uw, dw)


def grads_kernel(t_in, g_in, h_in, gd_in, ud_in, gg, ug, dg, tv, gv, hv, gdv, udv, ggv, ugv, dgv, lsems, csems, osems):
    lefts, pairs = [], []
    for k in PARTS:
        lefts.append(
            [
                pltpu.make_async_copy(src.at[k], dst.at[k], lsems.at[k * 3 + i])
                for i, (src, dst) in enumerate(((gd_in, gdv), (ud_in, udv), (h_in, hv)))
            ]
        )
        for copy in lefts[k]:
            copy.start()
        for half in range(2):
            cols = pl.ds(half * HALF + FROM[k], WIDE[k])
            at = (k * 2 + half) * 2
            pair = [
                pltpu.make_async_copy(t_in.at[:, cols], tv.at[:, cols], csems.at[at]),
                pltpu.make_async_copy(g_in.at[:, cols], gv.at[:, cols], csems.at[at + 1]),
            ]
            for copy in pair:
                copy.start()
            pairs.append(pair)
    outs = []
    for k in PARTS:
        for copy in lefts[k]:
            copy.wait()
        turned = [left[k].T for left in (gdv, udv, hv)]
        for half in range(2):
            cols = pl.ds(half * HALF + FROM[k], WIDE[k])
            for copy in pairs[k * 2 + half]:
                copy.wait()
            for left, right, mid, dst in zip(turned, (tv, tv, gv), (ggv, ugv, dgv), (gg, ug, dg)):
                mid[:, cols] = nn(left, right[:, cols]).astype(BF)
                out = pltpu.make_async_copy(mid.at[:, cols], dst.at[0, :, cols], osems.at[len(outs)])
                out.start()
                outs.append(out)
    for out in outs:
        out.wait()


def run_grads(t_rows, g_rows, h, gd, ud):
    anywhere = pl.BlockSpec(memory_space=pl.ANY)
    vm = pltpu.VMEM
    dma = pltpu.SemaphoreType.DMA
    return pl.pallas_call(
        grads_kernel,
        out_shape=(jax.ShapeDtypeStruct((1, HID, 2 * HALF), BF),) * 3,
        in_specs=[anywhere] * 5,
        out_specs=(anywhere,) * 3,
        scratch_shapes=[vm((512, 2 * HALF), BF)] * 2
        + [vm((3, 512, HID), BF)] * 3
        + [vm((HID, 2 * HALF), BF)] * 3
        + [dma((9,)), dma((12,)), dma((18,))],
        compiler_params=pltpu.CompilerParams(vmem_limit_bytes=62 * 2**20),
        cost_estimate=pl.CostEstimate(flops=5 * 10**9, bytes_accessed=2 * 10**7, transcendentals=0),
    )(t_rows, g_rows, h, gd, ud)


def shards(tokens, route_ids, route_weight, gate_weight, up_weight, down_weight, out_grad):
    mixed, tgrad, rg, t_rows, g_rows, h, gd, ud = run_main(
        tokens, out_grad, route_ids.T, route_weight.T, gate_weight, up_weight, down_weight
    )
    gate_grad, up_grad, down_grad = run_grads(t_rows, g_rows, h, gd, ud)
    return (mixed, tgrad, rg.T, gate_grad, up_grad, down_grad)


def solution(mesh):
    placed = (
        P("expert", "tensor"),
        P("expert", None),
        P("expert", None),
        P("expert", "tensor", None),
        P("expert", "tensor", None),
        P("expert", "tensor", None),
        P("expert", "tensor"),
    )
    return jax.shard_map(
        shards,
        mesh=mesh,
        in_specs=placed,
        out_specs=(
            P("expert", "tensor"),
            P("expert", "tensor"),
            P("expert", None),
            P("expert", "tensor", None),
            P("expert", "tensor", None),
            P("expert", "tensor", None),
        ),
        check_vma=False,
    )
```

```python
import jax
import jax.numpy as jnp
from jax import lax
from jax.experimental import pallas as pl
from jax.experimental.pallas import tpu as pltpu
from jax.sharding import PartitionSpec as P

MESH = pl.DeviceIdType.MESH
BF = jnp.bfloat16
F32 = jnp.float32
ROUTES = ((0, 1, 2), (2, 0, 1), (1, 2, 0))
STRIDE = (16, 4, 1)
WIDE = (768, 768, 512)
FROM = (0, 768, 1536)
HALF = 2048
HID = 384
PARTS = range(3)


def nt(left, right):
    return lax.dot_general(left, right, (((1,), (1,)), ((), ())), preferred_element_type=F32)


def tn(left, right):
    return lax.dot_general(left, right, (((0,), (0,)), ((), ())), preferred_element_type=F32)


def nn(left, right):
    return jnp.dot(left, right, preferred_element_type=F32)


class Group:
    def __init__(self, index, send_sem, recv_sem, whole, device):
        self.index, self.send_sem, self.recv_sem, self.open = index, send_sem, recv_sem, True
        self.all = pltpu.make_async_remote_copy(
            src_ref=whole, dst_ref=whole, send_sem=send_sem, recv_sem=recv_sem, device_id=device, device_id_type=MESH
        )

    def start(self, src, dst, device):
        pltpu.make_async_remote_copy(
            src_ref=src, dst_ref=dst, send_sem=self.send_sem, recv_sem=self.recv_sem, device_id=device, device_id_type=MESH
        ).start()

    def arrived(self):
        self.all.wait_recv()

    def sent(self):
        if self.open:
            self.all.wait_send()
        self.open = False


class Copies:
    def __init__(self, send_sems, recv_sems, device):
        self.send_sems, self.recv_sems, self.device, self.groups = send_sems, recv_sems, device, []

    def group(self, whole):
        i = len(self.groups)
        self.groups.append(Group(i, self.send_sems.at[i], self.recv_sems.at[i], whole, self.device))
        return self.groups[i]

    def one(self, src, dst, device):
        group = self.group(src)
        group.start(src, dst, device)
        return group

    def finish(self):
        for group in self.groups:
            group.sent()


def main_kernel(*refs):
    refs = list(refs)

    def take(n):
        got = refs[:n]
        del refs[:n]
        return got

    tok, og, ids_in, wts_in, gw, uw, dw = take(7)
    mixed, tgrad, rgo, t_out, g_out, h_out, gd_out, ud_out = take(8)
    (tab,) = take(1)
    ag = [take(3), take(3)]
    send = [take(3), take(3)]
    own = [take(3), take(3)]
    oth = [take(3), take(3)]
    tabs = take(3)
    pick = take(3)
    pickw = take(3)
    wcol = take(3)
    both = [take(3) for _ in range(3)]
    rest = [take(3) for _ in range(3)]
    part = take(3)
    gact, uact, fa, fb = take(4)
    hid = take(3)
    gdel = take(3)
    udel = take(3)
    qbuf, qsib, qrec, rgsend, rg2, rg1send, rg1 = take(7)
    crecv = [take(3), take(3)]
    prec = [take(3), take(3)]
    p1send = [take(3), take(3)]
    p1rec = [take(3), take(3)]
    send_sems, recv_sems, wsems, osems = take(4)

    me = lax.axis_index("expert")
    t = lax.axis_index("tensor")
    c = (me // 16, (me // 4) % 4, me % 4)
    sib = (me, 1 - t)
    remote = Copies(send_sems, recv_sems, sib)

    def at(dim, j):
        return lax.rem(c[dim] + j, 4)

    def peer(dim, j):
        return (me + (at(dim, j) - c[dim]) * STRIDE[dim], t)

    def rows(i, n):
        return pl.ds(pl.multiple_of(i * n, n), n)

    def expert_at(d3, d):
        return (me + (d - c[d3]) * STRIDE[d3]).astype(F32)

    barrier = pltpu.get_barrier_semaphore()
    for dim in PARTS:
        for j in (1, 2, 3):
            pl.semaphore_signal(barrier, inc=1, device_id=peer(dim, j), device_id_type=MESH)
    pl.semaphore_signal(barrier, inc=1, device_id=sib, device_id_type=MESH)

    loads = []
    for w, src in enumerate((gw, uw, dw)):
        for k in PARTS:
            mine = pl.ds(pl.multiple_of(t * HALF + FROM[k], 128), WIDE[k])
            other = pl.ds(pl.multiple_of((1 - t) * HALF + FROM[k], 128), WIDE[k])
            pltpu.make_async_copy(src.at[0, :, other], rest[w][k], wsems.at[w]).start()
            pltpu.make_async_copy(src.at[0, :, mine], both[w][k].at[pl.ds(0, HID)], wsems.at[w]).start()
        loads.append(pltpu.make_async_copy(src, src, wsems.at[w]))

    tab[0:8, :] = jnp.concatenate([ids_in[...].astype(F32)] * 4, axis=1)
    tab[8:16, :] = jnp.concatenate([wts_in[...]] * 4, axis=1)
    for k in PARTS:
        d1, d2, _ = ROUTES[k]
        tabs[k][c[d2], c[d1]] = tab[...]
        for s, src in enumerate((tok, og)):
            ag[s][k][rows(c[d2] * 4 + c[d1], 32), :] = src[:, pl.ds(FROM[k], WIDE[k])]
    pl.semaphore_wait(barrier, 10)

    first = [[], []]
    first_tab = []
    for k in PARTS:
        d1, d2, _ = ROUTES[k]
        first_tab.append(remote.group(tabs[k].at[0, pl.ds(0, 3)]))
        for j in (2, 1, 3):
            first_tab[k].start(tab, tabs[k].at[c[d2], c[d1]], peer(d1, j))
    for s, src in enumerate((tok, og)):
        for k in PARTS:
            d1, d2, _ = ROUTES[k]
            cols = pl.ds(FROM[k], WIDE[k])
            here = rows(c[d2] * 4 + c[d1], 32)
            first[s].append(remote.group(ag[s][k].at[pl.ds(0, 96)]))
            for j in (2, 1, 3):
                first[s][k].start(src.at[:, cols], ag[s][k].at[here], peer(d1, j))

    def second(s, k):
        first[s][k].arrived()
        d2 = ROUTES[k][1]
        block = ag[s][k].at[rows(c[d2], 128)]
        return {
            1: remote.one(block, block, peer(d2, 1)),
            3: remote.one(block, block, peer(d2, 3)),
            2: remote.group(block),
        }

    def relay(s, k, j):
        d2 = ROUTES[k][1]
        seconds[s][k][j].arrived()
        half = ag[s][k].at[rows(at(d2, 4 - j) * 2 + j // 2, 64)]
        seconds[s][k][2].start(half, half, peer(d2, j))

    lane16 = lax.broadcasted_iota(jnp.int32, (16, 128), 1) // 32
    tri_r = lax.broadcasted_iota(jnp.int32, (128, 128), 0)
    tri_c = lax.broadcasted_iota(jnp.int32, (128, 128), 1)
    before = jnp.where((tri_r // 32 == tri_c // 32) & (tri_r < tri_c), 1.0, 0.0).astype(BF)
    slot_row = lax.broadcasted_iota(jnp.int32, (32, 128), 0).astype(F32)
    lane8 = lax.broadcasted_iota(jnp.int32, (8, 128), 1) // 32
    block_base = (lane8 * 8).astype(F32)
    sub8 = lax.broadcasted_iota(jnp.int32, (8, 128), 0)

    def table(k, c2):
        tile = tabs[k][c2, 0]
        for c1 in range(1, 4):
            tile = jnp.where(lane16 == c1, tabs[k][c2, c1], tile)
        return tile[:8], tile[8:]

    def tables(k, c2):
        d3 = ROUTES[k][2]
        ids, wts = table(k, c2)
        hits = jnp.zeros((8, 128), F32)
        wds = []
        for d in range(4):
            same = ids == expert_at(d3, d)
            hits = jnp.where(sub8 == d, jnp.sum(jnp.where(same, 1.0, 0.0), axis=0, keepdims=True), hits)
            wds.append(jnp.sum(jnp.where(same, wts, 0.0), axis=0, keepdims=True))
        key = jnp.where(hits > 0.0, nn(hits.astype(BF), before) + block_base, -1.0)
        hit = [key[d : d + 1, :] == slot_row for d in range(4)]
        weight = jnp.concatenate([jnp.where(hit[d], wds[d], 0.0) for d in range(4)], axis=0)
        group = rows(c2, 128)
        pick[k][group, :] = jnp.concatenate([jnp.where(h, 1.0, 0.0) for h in hit], axis=0).astype(BF)
        pickw[k][group, :] = weight.astype(BF)
        wcol[k][group, :] = jnp.sum(weight, axis=1, keepdims=True)

    def third(s, k, j):
        _, d2, d3 = ROUTES[k]
        c2 = at(d2, j)
        group = rows(c2, 128)
        got = nn(pick[k][group, :], ag[s][k][group, :])
        if s == 1:
            got = got * wcol[k][group, :]
        send[s][k][group, :] = got.astype(BF)
        here = rows(c[d3] * 4 + c2, 32)
        for j3 in (2, 1, 3):
            thirds[s][k][j3].start(send[s][k].at[rows(c2 * 4 + at(d3, j3), 32)], own[s][k].at[here], peer(d3, j3))
        own[s][k][here, :] = send[s][k][rows(c2 * 4 + c[d3], 32), :]

    def forward(s, k):
        d3 = ROUTES[k][2]
        out = remote.group(oth[s][k])
        for j3 in (0, 1, 3, 2):
            if j3:
                thirds[s][k][j3].arrived()
            r = rows(at(d3, 4 - j3), 128)
            out.start(own[s][k].at[r], oth[s][k].at[r], sib)
        return out

    thirds = [[{j3: remote.group(own[s][k].at[pl.ds(0, 128)]) for j3 in (1, 2, 3)} for k in PARTS] for s in range(2)]
    seconds, second_tab = [[], []], []
    for k in PARTS:
        first_tab[k].arrived()
        d2 = ROUTES[k][1]
        second_tab.append({j: remote.one(tabs[k].at[c[d2]], tabs[k].at[c[d2]], peer(d2, j)) for j in (2, 1, 3)})
    for k in PARTS:
        seconds[0].append(second(0, k))
    for k in PARTS:
        tables(k, c[ROUTES[k][1]])
        third(0, k, 0)

    for load in loads:
        load.wait()
    swaps = [[remote.one(rest[w][k], both[w][k].at[pl.ds(HID, HID)], sib) for k in PARTS] for w in range(3)]

    for j in (1, 3):
        for k in PARTS:
            relay(0, k, j)
        for k in PARTS:
            second_tab[k][j].arrived()
            tables(k, at(ROUTES[k][1], 4 - j))
            third(0, k, 4 - j)
    for k in PARTS:
        seconds[1].append(second(1, k))
    for k in PARTS:
        second_tab[k][2].arrived()
        tables(k, at(ROUTES[k][1], 2))
        seconds[0][k][2].arrived()
        third(0, k, 2)
    for k in PARTS:
        third(1, k, 0)

    def store(src, dst, i):
        pltpu.make_async_copy(src, dst, osems.at[i]).start()

    def keep_rows(s, k, dst):
        mine = pl.ds(pl.multiple_of(t * HALF + FROM[k], 128), WIDE[k])
        other = pl.ds(pl.multiple_of((1 - t) * HALF + FROM[k], 128), WIDE[k])
        store(own[s][k], dst.at[:, mine], s)
        store(oth[s][k], dst.at[:, other], s)

    def spot(k, x, y, z):
        v = (z, y, x)
        d1, d2, d3 = ROUTES[k]
        return pl.ds(pl.multiple_of(((v[d3] * 4 + v[d2]) * 4 + v[d1]) * 8, 8), 8)

    def contract_own(s, w, k):
        part[k][...] = nt(own[s][k][...], both[w][k][pl.ds(0, HID), :])

    def contract_oth(s, w, k):
        part[k][...] += nt(oth[s][k][...], rest[w][k][...])

    def gather_parts(dst):
        def body(i, carry):
            y, z = i // 4, i % 4
            for x in range(4):
                dst[spot(0, x, y, z), :] = (
                    part[0][spot(0, x, y, z), :] + part[1][spot(1, x, y, z), :] + part[2][spot(2, x, y, z), :]
                )
            return carry

        lax.fori_loop(0, 16, body, 0)

    def spread(src, dst, k):
        if k == 0:
            dst[:, pl.ds(0, HID)] = src[...].astype(BF)
            return

        def body(i, carry):
            a, b = i // 4, i % 4
            spots = [spot(0, n, a, b) if k == 1 else spot(0, b, n, a) for n in range(4)]
            dst[rows(i, 32), pl.ds(0, HID)] = jnp.concatenate([src[at, :] for at in spots], axis=0).astype(BF)
            return carry

        lax.fori_loop(0, 16, body, 0)

    def swap_cols(dst):
        return remote.one(dst.at[:, pl.ds(0, HID)], dst.at[:, pl.ds(HID, HID)], sib)

    cross_tok = []
    for k in PARTS:
        cross_tok.append(forward(0, k))
        contract_own(0, 0, k)
    for k in PARTS:
        cross_tok[k].arrived()
        keep_rows(0, k, t_out)
        contract_oth(0, 0, k)
    gather_parts(gact)
    for j in (1, 3):
        for k in PARTS:
            relay(1, k, j)
        for k in PARTS:
            third(1, k, 4 - j)
    for k in PARTS:
        contract_own(0, 1, k)
        contract_oth(0, 1, k)
    for k in PARTS:
        seconds[1][k][2].arrived()
        third(1, k, 2)
    gather_parts(uact)
    gate = gact[...]
    fa[...] = gate * jax.nn.sigmoid(gate) * uact[...]
    cross_hid = []
    for k in PARTS:
        spread(fa, hid[k], k)
        cross_hid.append(swap_cols(hid[k]))
    for k in PARTS:
        store(hid[k].at[:, pl.ds(0, HID)], h_out.at[k], 2)

    def reuse(s, k):
        for j in (1, 2, 3):
            seconds[s][k][j].sent()
            thirds[s][k][j].sent()

    def back3(s, k):
        _, d2, d3 = ROUTES[k]
        out = {}
        for j in (2, 1, 3, 0):
            c2 = at(d2, j)
            here = rows(c2 * 4 + c[d3], 32)
            out[j] = remote.group(crecv[s][k].at[pl.ds(0, 96)])
            for j3 in (2, 1, 3):
                out[j].start(send[s][k].at[rows(at(d3, j3) * 4 + c2, 32)], crecv[s][k].at[here], peer(d3, j3))
            crecv[s][k][here, :] = send[s][k][rows(c[d3] * 4 + c2, 32), :]
        return out

    def back2(s, thirds_back):
        out = [remote.group(prec[s][k]) for k in PARTS]
        for j in (2, 1, 3, 0):
            for k in PARTS:
                d2 = ROUTES[k][1]
                thirds_back[k][j].arrived()
                group = rows(at(d2, j), 128)
                ag[s][k][group, :] = tn((pickw, pick)[s][k][group, :], crecv[s][k][group, :]).astype(BF)
                if j:
                    out[k].start(ag[s][k].at[group], prec[s][k].at[j - 1], peer(d2, j))
        return out

    def back1(s, k, seconds_back):
        seconds_back.arrived()
        d1, d2, _ = ROUTES[k]
        total = ag[s][k][rows(c[d2], 128), :].astype(F32)
        for j in range(3):
            total = total + prec[s][k][j].astype(F32)
        p1send[s][k][...] = total.astype(BF)
        out = remote.group(p1rec[s][k])
        for j in (2, 1, 3):
            out.start(p1send[s][k].at[rows(at(d1, j), 32)], p1rec[s][k].at[j - 1], peer(d1, j))
        return out

    def back0(s, k, firsts_back, dst):
        firsts_back.arrived()
        total = p1send[s][k][rows(c[ROUTES[k][0]], 32), :].astype(F32)
        for j in range(3):
            total = total + p1rec[s][k][j].astype(F32)
        dst[:, pl.ds(FROM[k], WIDE[k])] = total.astype(BF)

    out3 = []
    for k in PARTS:
        swaps[2][k].arrived()
        cross_hid[k].arrived()
        reuse(0, k)
        send[0][k][...] = nn(hid[k][...], both[2][k][...]).astype(BF)
        out3.append(back3(0, k))

    cross_og = []
    for k in PARTS:
        cross_og.append(forward(1, k))
        contract_own(1, 2, k)
    for k in PARTS:
        cross_og[k].arrived()
        keep_rows(1, k, g_out)
        contract_oth(1, 2, k)
    gather_parts(fb)
    gate = gact[...]
    sg = jax.nn.sigmoid(gate)
    grad = fb[...]
    qprod = fa[...].astype(BF).astype(F32) * grad
    fa[...] = grad * uact[...] * sg * (1.0 + gate * (1.0 - sg))
    fb[...] = grad * (gate * sg)
    cross_gd, cross_ud = [], []
    for k in PARTS:
        spread(fa, gdel[k], k)
        cross_gd.append(swap_cols(gdel[k]))
        spread(fb, udel[k], k)
        cross_ud.append(swap_cols(udel[k]))
    qbuf[...] = lax.dot_general(
        jnp.ones((8, HID), F32), qprod, (((1,), (1,)), ((), ())), precision=lax.Precision.HIGHEST, preferred_element_type=F32
    )
    cross_q = remote.one(qbuf, qsib, sib)
    for k in PARTS:
        store(gdel[k].at[:, pl.ds(0, HID)], gd_out.at[k], 3)
        store(udel[k].at[:, pl.ds(0, HID)], ud_out.at[k], 4)

    out2 = back2(0, out3)

    bk3 = []
    for k in PARTS:
        for w in range(2):
            swaps[w][k].arrived()
        cross_gd[k].arrived()
        cross_ud[k].arrived()
        reuse(1, k)
        send[1][k][...] = (nn(gdel[k][...], both[0][k][...]) + nn(udel[k][...], both[1][k][...])).astype(BF)
        bk3.append(back3(1, k))

    d1, d2, d3 = ROUTES[0]
    cross_q.arrived()
    q = qbuf[...] + qsib[...]
    for i in range(4):
        rgsend[i] = q[:, i * 128 : i * 128 + 128]
    rg3 = remote.group(qrec.at[pl.ds(0, 3)])
    for j in (2, 1, 3):
        rg3.start(rgsend.at[at(d3, j)], qrec.at[c[d3]], peer(d3, j))
    qrec[c[d3]] = rgsend[c[d3]]

    out1 = [back1(0, k, out2[k]) for k in PARTS]

    rg3.arrived()
    rg3.sent()
    for c2 in range(4):
        ids, wts = table(0, c2)
        spots = jnp.concatenate([qrec[d][:, c2 * 32 : c2 * 32 + 32] for d in range(4)], axis=1)
        values = jnp.dot(
            jnp.where(sub8 == lane8, spots, 0.0),
            pick[0][pl.ds(c2 * 128, 128), :].astype(F32),
            precision=lax.Precision.HIGHEST,
            preferred_element_type=F32,
        )
        rg = jnp.zeros((8, 128), F32)
        for d in range(4):
            rg = rg + jnp.where(ids == expert_at(d3, d), values[d : d + 1, :], 0.0)
        rgsend[c2] = rg / wts
    rgc2 = remote.group(rg2)
    for j in (2, 1, 3):
        rgc2.start(rgsend.at[at(d2, j)], rg2.at[j - 1], peer(d2, j))

    bk2 = back2(1, bk3)
    rgc2.arrived()
    rg1send[...] = rgsend[c[d2]] + rg2[0] + rg2[1] + rg2[2]
    rgc1 = remote.group(rg1)
    for j in (2, 1, 3):
        rgc1.start(rg1send, rg1.at[j - 1], peer(d1, j))
    for k in PARTS:
        back0(0, k, out1[k], mixed)
    rgc1.arrived()
    rg = rg1send[...] + rg1[0] + rg1[1] + rg1[2]
    mine = rg[:, 0:32]
    for i in range(1, 4):
        mine = jnp.where(c[d1] == i, rg[:, i * 32 : i * 32 + 32], mine)
    rgo[...] = mine
    bk1 = [back1(1, k, bk2[k]) for k in PARTS]
    for i, dst in enumerate((t_out, g_out, h_out, gd_out, ud_out)):
        pltpu.make_async_copy(dst, dst, osems.at[i]).wait()
    for k in PARTS:
        back0(1, k, bk1[k], tgrad)
    remote.finish()


N_GROUPS = 124


def run_main(tok, og, ids, wts, gw, uw, dw):
    vm = pltpu.VMEM
    scratch = [vm((16, 128), F32)]

    def per(make):
        scratch.extend(make(WIDE[k]) for k in PARTS)

    for _ in range(8):
        per(lambda w: vm((512, w), BF))
    per(lambda w: vm((4, 4, 16, 128), F32))
    per(lambda w: vm((512, 128), BF))
    per(lambda w: vm((512, 128), BF))
    per(lambda w: vm((512, 1), F32))
    for _ in range(3):
        per(lambda w: vm((2 * HID, w), BF))
    for _ in range(3):
        per(lambda w: vm((HID, w), BF))
    per(lambda w: vm((512, HID), F32))
    scratch.extend(vm((512, HID), F32) for _ in range(4))
    for _ in range(3):
        per(lambda w: vm((512, 2 * HID), BF))
    scratch.extend(vm(s, F32) for s in ((8, 512), (8, 512), (4, 8, 128), (4, 8, 128), (3, 8, 128), (8, 128), (3, 8, 128)))
    for _ in range(2):
        per(lambda w: vm((512, w), BF))
    for _ in range(2):
        per(lambda w: vm((3, 128, w), BF))
    for _ in range(2):
        per(lambda w: vm((128, w), BF))
    for _ in range(2):
        per(lambda w: vm((3, 32, w), BF))
    scratch.extend(
        [
            pltpu.SemaphoreType.DMA((N_GROUPS,)),
            pltpu.SemaphoreType.DMA((N_GROUPS,)),
            pltpu.SemaphoreType.DMA((3,)),
            pltpu.SemaphoreType.DMA((5,)),
        ]
    )
    in_vmem = pl.BlockSpec(memory_space=pltpu.VMEM)
    anywhere = pl.BlockSpec(memory_space=pl.ANY)
    shape = jax.ShapeDtypeStruct
    return pl.pallas_call(
        main_kernel,
        out_shape=(
            shape((32, HALF), BF),
            shape((32, HALF), BF),
            shape((8, 32), F32),
            shape((512, 2 * HALF), BF),
            shape((512, 2 * HALF), BF),
            shape((3, 512, HID), BF),
            shape((3, 512, HID), BF),
            shape((3, 512, HID), BF),
        ),
        in_specs=[in_vmem] * 4 + [anywhere] * 3,
        out_specs=(in_vmem,) * 3 + (anywhere,) * 5,
        scratch_shapes=scratch,
        compiler_params=pltpu.CompilerParams(collective_id=0, has_side_effects=True, vmem_limit_bytes=63 * 2**20),
        cost_estimate=pl.CostEstimate(flops=10**10, bytes_accessed=2 * 10**7, transcendentals=10**6),
    )(tok, og, ids, wts, gw, uw, dw)


def grads_kernel(
    t_in, g_in, h_in, gd_in, ud_in, mixed_in, tgrad_in, rg_in,
    gg, ug, dg, mixed, tgrad, rg,
    tv, gv, hv, gdv, udv, ggv, ugv, dgv, lsems, csems, osems, psems
):
    passing = [
        pltpu.make_async_copy(src, dst, psems.at[i])
        for i, (src, dst) in enumerate(((mixed_in, mixed), (tgrad_in, tgrad), (rg_in, rg)))
    ]
    lefts, pairs = [], []
    for k in PARTS:
        lefts.append(
            [
                pltpu.make_async_copy(src.at[k], dst.at[k], lsems.at[k * 3 + i])
                for i, (src, dst) in enumerate(((gd_in, gdv), (ud_in, udv), (h_in, hv)))
            ]
        )
        for copy in lefts[k]:
            copy.start()
        for half in range(2):
            cols = pl.ds(half * HALF + FROM[k], WIDE[k])
            at = (k * 2 + half) * 2
            pair = [
                pltpu.make_async_copy(t_in.at[:, cols], tv.at[:, cols], csems.at[at]),
                pltpu.make_async_copy(g_in.at[:, cols], gv.at[:, cols], csems.at[at + 1]),
            ]
            for copy in pair:
                copy.start()
            pairs.append(pair)
    for copy in passing:
        copy.start()
    outs = []
    for k in PARTS:
        for copy in lefts[k]:
            copy.wait()
        pair_t = jnp.concatenate([gdv[k].T, udv[k].T], axis=0)
        hid_t = hv[k].T
        for half in range(2):
            cols = pl.ds(half * HALF + FROM[k], WIDE[k])
            for copy in pairs[k * 2 + half]:
                copy.wait()
            two = nn(pair_t, tv[:, cols]).astype(BF)
            ggv[:, cols] = two[:HID]
            ugv[:, cols] = two[HID:]
            dgv[:, cols] = nn(hid_t, gv[:, cols]).astype(BF)
            for mid, dst in zip((ggv, ugv, dgv), (gg, ug, dg)):
                out = pltpu.make_async_copy(mid.at[:, cols], dst.at[0, :, cols], osems.at[len(outs)])
                out.start()
                outs.append(out)
    for out in outs + passing:
        out.wait()


def run_grads(t_rows, g_rows, h, gd, ud, mixed, tgrad, rg):
    anywhere = pl.BlockSpec(memory_space=pl.ANY)
    vm = pltpu.VMEM
    dma = pltpu.SemaphoreType.DMA
    shape = jax.ShapeDtypeStruct
    return pl.pallas_call(
        grads_kernel,
        out_shape=(shape((1, HID, 2 * HALF), BF),) * 3
        + tuple(shape(x.shape, x.dtype) for x in (mixed, tgrad, rg)),
        in_specs=[anywhere] * 8,
        out_specs=(anywhere,) * 6,
        scratch_shapes=[vm((512, 2 * HALF), BF)] * 2
        + [vm((3, 512, HID), BF)] * 3
        + [vm((HID, 2 * HALF), BF)] * 3
        + [dma((9,)), dma((12,)), dma((18,)), dma((3,))],
        compiler_params=pltpu.CompilerParams(vmem_limit_bytes=62 * 2**20),
        cost_estimate=pl.CostEstimate(flops=5 * 10**9, bytes_accessed=2 * 10**7, transcendentals=0),
    )(t_rows, g_rows, h, gd, ud, mixed, tgrad, rg)


def shards(tokens, route_ids, route_weight, gate_weight, up_weight, down_weight, out_grad):
    mixed, tgrad, rg, t_rows, g_rows, h, gd, ud = run_main(
        tokens, out_grad, route_ids.T, route_weight.T, gate_weight, up_weight, down_weight
    )
    gate_grad, up_grad, down_grad, mixed, tgrad, rg = run_grads(t_rows, g_rows, h, gd, ud, mixed, tgrad, rg)
    return (mixed, tgrad, rg.T, gate_grad, up_grad, down_grad)


def solution(mesh):
    placed = (
        P("expert", "tensor"),
        P("expert", None),
        P("expert", None),
        P("expert", "tensor", None),
        P("expert", "tensor", None),
        P("expert", "tensor", None),
        P("expert", "tensor"),
    )
    return jax.shard_map(
        shards,
        mesh=mesh,
        in_specs=placed,
        out_specs=(
            P("expert", "tensor"),
            P("expert", "tensor"),
            P("expert", None),
            P("expert", "tensor", None),
            P("expert", "tensor", None),
            P("expert", "tensor", None),
        ),
        check_vma=False,
    )
```

```python
import jax
import jax.numpy as jnp
from jax import lax
from jax.experimental import pallas as pl
from jax.experimental.pallas import tpu as pltpu
from jax.sharding import PartitionSpec as P

MESH = pl.DeviceIdType.MESH
BF = jnp.bfloat16
F32 = jnp.float32
ROUTES = ((0, 1, 2), (2, 0, 1), (1, 2, 0))
STRIDE = (16, 4, 1)
WIDE = (768, 768, 512)
FROM = (0, 768, 1536)
HALF = 2048
HID = 384
PARTS = range(3)


def nt(left, right):
    return lax.dot_general(left, right, (((1,), (1,)), ((), ())), preferred_element_type=F32)


def tn(left, right):
    return lax.dot_general(left, right, (((0,), (0,)), ((), ())), preferred_element_type=F32)


def nn(left, right):
    return jnp.dot(left, right, preferred_element_type=F32)


class Group:
    def __init__(self, index, send_sem, recv_sem, whole, device):
        self.index, self.send_sem, self.recv_sem, self.open = index, send_sem, recv_sem, True
        self.all = pltpu.make_async_remote_copy(
            src_ref=whole, dst_ref=whole, send_sem=send_sem, recv_sem=recv_sem, device_id=device, device_id_type=MESH
        )

    def start(self, src, dst, device):
        pltpu.make_async_remote_copy(
            src_ref=src, dst_ref=dst, send_sem=self.send_sem, recv_sem=self.recv_sem, device_id=device, device_id_type=MESH
        ).start()

    def arrived(self):
        self.all.wait_recv()

    def sent(self):
        if self.open:
            self.all.wait_send()
        self.open = False


class Copies:
    def __init__(self, send_sems, recv_sems, device):
        self.send_sems, self.recv_sems, self.device, self.groups = send_sems, recv_sems, device, []

    def group(self, whole):
        i = len(self.groups)
        self.groups.append(Group(i, self.send_sems.at[i], self.recv_sems.at[i], whole, self.device))
        return self.groups[i]

    def one(self, src, dst, device):
        group = self.group(src)
        group.start(src, dst, device)
        return group

    def finish(self):
        for group in self.groups:
            group.sent()


def main_kernel(*refs):
    refs = list(refs)

    def take(n):
        got = refs[:n]
        del refs[:n]
        return got

    tok, og, ids_in, wts_in, gw, uw, dw = take(7)
    mixed, tgrad, rgo, t_out, g_out, h_out, gd_out, ud_out = take(8)
    (tab,) = take(1)
    ag = [take(3), take(3)]
    send = [take(3), take(3)]
    own = [take(3), take(3)]
    oth = [take(3), take(3)]
    (tabs_all,) = take(1)
    tabs = [tabs_all.at[k] for k in PARTS]
    pick = take(3)
    pickw = take(3)
    wcol = take(3)
    both = [take(3) for _ in range(3)]
    rest = [take(3) for _ in range(3)]
    part = take(3)
    gact, uact, fa, fb = take(4)
    hid = take(3)
    gdel = take(3)
    udel = take(3)
    qbuf, qsib, qrec, rgsend, rg2, rg1send, rg1 = take(7)
    crecv = [take(3), take(3)]
    prec = [take(3), take(3)]
    p1send = [take(3), take(3)]
    p1rec = [take(3), take(3)]
    send_sems, recv_sems, wsems, osems = take(4)

    me = lax.axis_index("expert")
    t = lax.axis_index("tensor")
    c = (me // 16, (me // 4) % 4, me % 4)
    sib = (me, 1 - t)
    remote = Copies(send_sems, recv_sems, sib)

    def at(dim, j):
        return lax.rem(c[dim] + j, 4)

    def peer(dim, j):
        return (me + (at(dim, j) - c[dim]) * STRIDE[dim], t)

    def rows(i, n):
        return pl.ds(pl.multiple_of(i * n, n), n)

    def expert_at(d3, d):
        return (me + (d - c[d3]) * STRIDE[d3]).astype(F32)

    barrier = pltpu.get_barrier_semaphore()
    for dim in PARTS:
        for j in (1, 2, 3):
            pl.semaphore_signal(barrier, inc=1, device_id=peer(dim, j), device_id_type=MESH)
    pl.semaphore_signal(barrier, inc=1, device_id=sib, device_id_type=MESH)

    loads = []
    for w, src in enumerate((gw, uw, dw)):
        for k in PARTS:
            mine = pl.ds(pl.multiple_of(t * HALF + FROM[k], 128), WIDE[k])
            other = pl.ds(pl.multiple_of((1 - t) * HALF + FROM[k], 128), WIDE[k])
            pltpu.make_async_copy(src.at[0, :, other], rest[w][k], wsems.at[w]).start()
            pltpu.make_async_copy(src.at[0, :, mine], both[w][k].at[pl.ds(0, HID)], wsems.at[w]).start()
        loads.append(pltpu.make_async_copy(src, src, wsems.at[w]))

    tab[0:8, :] = jnp.concatenate([ids_in[...].astype(F32)] * 4, axis=1)
    tab[8:16, :] = jnp.concatenate([wts_in[...]] * 4, axis=1)
    for k in PARTS:
        d1, d2, _ = ROUTES[k]
        tabs[k][c[d2], c[d1]] = tab[...]
        for s, src in enumerate((tok, og)):
            ag[s][k][rows(c[d2] * 4 + c[d1], 32), :] = src[:, pl.ds(FROM[k], WIDE[k])]
    pl.semaphore_wait(barrier, 10)

    first = [[], []]
    first_tab = remote.group(tabs_all.at[:, 0, pl.ds(0, 3)])
    for k in PARTS:
        d1, d2, _ = ROUTES[k]
        for j in (2, 1, 3):
            first_tab.start(tab, tabs[k].at[c[d2], c[d1]], peer(d1, j))
    for s, src in enumerate((tok, og)):
        for k in PARTS:
            d1, d2, _ = ROUTES[k]
            cols = pl.ds(FROM[k], WIDE[k])
            here = rows(c[d2] * 4 + c[d1], 32)
            first[s].append(remote.group(ag[s][k].at[pl.ds(0, 96)]))
            for j in (2, 1, 3):
                first[s][k].start(src.at[:, cols], ag[s][k].at[here], peer(d1, j))

    def second(s, k):
        first[s][k].arrived()
        d2 = ROUTES[k][1]
        block = ag[s][k].at[rows(c[d2], 128)]
        return {
            1: remote.one(block, block, peer(d2, 1)),
            3: remote.one(block, block, peer(d2, 3)),
            2: remote.group(block),
        }

    def relay(s, k, j):
        d2 = ROUTES[k][1]
        seconds[s][k][j].arrived()
        half = ag[s][k].at[rows(at(d2, 4 - j) * 2 + j // 2, 64)]
        seconds[s][k][2].start(half, half, peer(d2, j))

    lane16 = lax.broadcasted_iota(jnp.int32, (16, 128), 1) // 32
    tri_r = lax.broadcasted_iota(jnp.int32, (128, 128), 0)
    tri_c = lax.broadcasted_iota(jnp.int32, (128, 128), 1)
    before = jnp.where((tri_r // 32 == tri_c // 32) & (tri_r < tri_c), 1.0, 0.0).astype(BF)
    slot_row = lax.broadcasted_iota(jnp.int32, (32, 128), 0).astype(F32)
    lane8 = lax.broadcasted_iota(jnp.int32, (8, 128), 1) // 32
    block_base = (lane8 * 8).astype(F32)
    sub8 = lax.broadcasted_iota(jnp.int32, (8, 128), 0)

    def table(k, c2):
        tile = tabs[k][c2, 0]
        for c1 in range(1, 4):
            tile = jnp.where(lane16 == c1, tabs[k][c2, c1], tile)
        return tile[:8], tile[8:]

    def tables(k, c2):
        d3 = ROUTES[k][2]
        ids, wts = table(k, c2)
        hits = jnp.zeros((8, 128), F32)
        wds = []
        for d in range(4):
            same = ids == expert_at(d3, d)
            hits = jnp.where(sub8 == d, jnp.sum(jnp.where(same, 1.0, 0.0), axis=0, keepdims=True), hits)
            wds.append(jnp.sum(jnp.where(same, wts, 0.0), axis=0, keepdims=True))
        key = jnp.where(hits > 0.0, nn(hits.astype(BF), before) + block_base, -1.0)
        hit = [key[d : d + 1, :] == slot_row for d in range(4)]
        weight = jnp.concatenate([jnp.where(hit[d], wds[d], 0.0) for d in range(4)], axis=0)
        group = rows(c2, 128)
        pick[k][group, :] = jnp.concatenate([jnp.where(h, 1.0, 0.0) for h in hit], axis=0).astype(BF)
        pickw[k][group, :] = weight.astype(BF)
        wcol[k][group, :] = jnp.sum(weight, axis=1, keepdims=True)

    def third(s, k, j):
        _, d2, d3 = ROUTES[k]
        c2 = at(d2, j)
        group = rows(c2, 128)
        got = nn(pick[k][group, :], ag[s][k][group, :])
        if s == 1:
            got = got * wcol[k][group, :]
        send[s][k][group, :] = got.astype(BF)
        here = rows(c[d3] * 4 + c2, 32)
        for j3 in (2, 1, 3):
            thirds[s][k][j3].start(send[s][k].at[rows(c2 * 4 + at(d3, j3), 32)], own[s][k].at[here], peer(d3, j3))
        own[s][k][here, :] = send[s][k][rows(c2 * 4 + c[d3], 32), :]

    def forward(s, k):
        d3 = ROUTES[k][2]
        out = remote.group(oth[s][k])
        for j3 in (0, 1, 3, 2):
            if j3:
                thirds[s][k][j3].arrived()
            r = rows(at(d3, 4 - j3), 128)
            out.start(own[s][k].at[r], oth[s][k].at[r], sib)
        return out

    thirds = [[{j3: remote.group(own[s][k].at[pl.ds(0, 128)]) for j3 in (1, 2, 3)} for k in PARTS] for s in range(2)]
    seconds = [[], []]
    second_tab = {j: remote.group(tabs_all.at[:, 0]) for j in (2, 1, 3)}
    first_tab.arrived()
    for k in PARTS:
        d2 = ROUTES[k][1]
        for j in (2, 1, 3):
            second_tab[j].start(tabs[k].at[c[d2]], tabs[k].at[c[d2]], peer(d2, j))
    for k in PARTS:
        seconds[0].append(second(0, k))
    for k in PARTS:
        tables(k, c[ROUTES[k][1]])
        third(0, k, 0)

    for load in loads:
        load.wait()
    swaps = [[remote.one(rest[w][k], both[w][k].at[pl.ds(HID, HID)], sib) for k in PARTS] for w in range(3)]

    for j in (1, 3):
        for k in PARTS:
            relay(0, k, j)
        second_tab[j].arrived()
        for k in PARTS:
            tables(k, at(ROUTES[k][1], 4 - j))
            third(0, k, 4 - j)
    for k in PARTS:
        seconds[1].append(second(1, k))
    second_tab[2].arrived()
    for k in PARTS:
        tables(k, at(ROUTES[k][1], 2))
        seconds[0][k][2].arrived()
        third(0, k, 2)
    for k in PARTS:
        third(1, k, 0)

    def store(src, dst, i):
        pltpu.make_async_copy(src, dst, osems.at[i]).start()

    def keep_rows(s, k, dst):
        mine = pl.ds(pl.multiple_of(t * HALF + FROM[k], 128), WIDE[k])
        other = pl.ds(pl.multiple_of((1 - t) * HALF + FROM[k], 128), WIDE[k])
        store(own[s][k], dst.at[:, mine], s)
        store(oth[s][k], dst.at[:, other], s)

    def spot(k, x, y, z):
        v = (z, y, x)
        d1, d2, d3 = ROUTES[k]
        return pl.ds(pl.multiple_of(((v[d3] * 4 + v[d2]) * 4 + v[d1]) * 8, 8), 8)

    def contract_own(s, w, k):
        part[k][...] = nt(own[s][k][...], both[w][k][pl.ds(0, HID), :])

    def contract_oth(s, w, k):
        part[k][...] += nt(oth[s][k][...], rest[w][k][...])

    def gather_parts(dst):
        def body(i, carry):
            y, z = i // 4, i % 4
            for x in range(4):
                dst[spot(0, x, y, z), :] = (
                    part[0][spot(0, x, y, z), :] + part[1][spot(1, x, y, z), :] + part[2][spot(2, x, y, z), :]
                )
            return carry

        lax.fori_loop(0, 16, body, 0)

    def spread(src, dst, k):
        if k == 0:
            dst[:, pl.ds(0, HID)] = src[...].astype(BF)
            return

        def body(i, carry):
            a, b = i // 4, i % 4
            spots = [spot(0, n, a, b) if k == 1 else spot(0, b, n, a) for n in range(4)]
            dst[rows(i, 32), pl.ds(0, HID)] = jnp.concatenate([src[at, :] for at in spots], axis=0).astype(BF)
            return carry

        lax.fori_loop(0, 16, body, 0)

    def swap_cols(dst):
        return remote.one(dst.at[:, pl.ds(0, HID)], dst.at[:, pl.ds(HID, HID)], sib)

    cross_tok = []
    for k in PARTS:
        cross_tok.append(forward(0, k))
        contract_own(0, 0, k)
    for j in (1, 3):
        for k in PARTS:
            relay(1, k, j)
    for k in PARTS:
        cross_tok[k].arrived()
        keep_rows(0, k, t_out)
        contract_oth(0, 0, k)
    gather_parts(gact)
    for j in (1, 3):
        for k in PARTS:
            third(1, k, 4 - j)
    for k in PARTS:
        contract_own(0, 1, k)
        contract_oth(0, 1, k)
    gather_parts(uact)
    gate = gact[...]
    fa[...] = gate * jax.nn.sigmoid(gate) * uact[...]
    cross_hid = []
    for k in PARTS:
        spread(fa, hid[k], k)
        cross_hid.append(swap_cols(hid[k]))
    for k in PARTS:
        store(hid[k].at[:, pl.ds(0, HID)], h_out.at[k], 2)

    for k in PARTS:
        seconds[1][k][2].arrived()
        third(1, k, 2)

    def reuse(s, k):
        for j in (1, 2, 3):
            seconds[s][k][j].sent()
            thirds[s][k][j].sent()

    def back3(s, k, out):
        _, d2, d3 = ROUTES[k]
        for j in (2, 1, 3, 0):
            c2 = at(d2, j)
            here = rows(c2 * 4 + c[d3], 32)
            for j3 in (2, 1, 3):
                out[j].start(send[s][k].at[rows(at(d3, j3) * 4 + c2, 32)], crecv[s][k].at[here], peer(d3, j3))
            crecv[s][k][here, :] = send[s][k][rows(c[d3] * 4 + c2, 32), :]

    def back2(s, thirds_back):
        out = [remote.group(prec[s][k]) for k in PARTS]
        for j in (2, 1, 3, 0):
            thirds_back[j].arrived()
            for k in PARTS:
                d2 = ROUTES[k][1]
                group = rows(at(d2, j), 128)
                ag[s][k][group, :] = tn((pickw, pick)[s][k][group, :], crecv[s][k][group, :]).astype(BF)
                if j:
                    out[k].start(ag[s][k].at[group], prec[s][k].at[j - 1], peer(d2, j))
        return out

    def back1(s, k, seconds_back):
        seconds_back.arrived()
        d1, d2, _ = ROUTES[k]
        total = ag[s][k][rows(c[d2], 128), :].astype(F32)
        for j in range(3):
            total = total + prec[s][k][j].astype(F32)
        p1send[s][k][...] = total.astype(BF)
        out = remote.group(p1rec[s][k])
        for j in (2, 1, 3):
            out.start(p1send[s][k].at[rows(at(d1, j), 32)], p1rec[s][k].at[j - 1], peer(d1, j))
        return out

    def back0(s, k, firsts_back, dst):
        firsts_back.arrived()
        total = p1send[s][k][rows(c[ROUTES[k][0]], 32), :].astype(F32)
        for j in range(3):
            total = total + p1rec[s][k][j].astype(F32)
        dst[:, pl.ds(FROM[k], WIDE[k])] = total.astype(BF)

    out3 = {j: remote.group(gw.at[0, pl.ds(0, 96), pl.ds(0, HALF)]) for j in (2, 1, 3, 0)}
    for k in PARTS:
        swaps[2][k].arrived()
        cross_hid[k].arrived()
        reuse(0, k)
        send[0][k][...] = nn(hid[k][...], both[2][k][...]).astype(BF)
        back3(0, k, out3)

    cross_og = []
    for k in PARTS:
        cross_og.append(forward(1, k))
        contract_own(1, 2, k)
    for k in PARTS:
        cross_og[k].arrived()
        keep_rows(1, k, g_out)
        contract_oth(1, 2, k)
    gather_parts(fb)
    gate = gact[...]
    sg = jax.nn.sigmoid(gate)
    grad = fb[...]
    qprod = fa[...].astype(BF).astype(F32) * grad
    fa[...] = grad * uact[...] * sg * (1.0 + gate * (1.0 - sg))
    fb[...] = grad * (gate * sg)
    cross_gd, cross_ud = [], []
    for k in PARTS:
        spread(fa, gdel[k], k)
        cross_gd.append(swap_cols(gdel[k]))
        spread(fb, udel[k], k)
        cross_ud.append(swap_cols(udel[k]))
    qbuf[...] = lax.dot_general(
        jnp.ones((8, HID), F32), qprod, (((1,), (1,)), ((), ())), precision=lax.Precision.HIGHEST, preferred_element_type=F32
    )
    cross_q = remote.one(qbuf, qsib, sib)
    for k in PARTS:
        store(gdel[k].at[:, pl.ds(0, HID)], gd_out.at[k], 3)
        store(udel[k].at[:, pl.ds(0, HID)], ud_out.at[k], 4)

    out2 = back2(0, out3)

    bk3 = {j: remote.group(gw.at[0, pl.ds(0, 96), pl.ds(0, HALF)]) for j in (2, 1, 3, 0)}
    for k in PARTS:
        for w in range(2):
            swaps[w][k].arrived()
        cross_gd[k].arrived()
        cross_ud[k].arrived()
        reuse(1, k)
        send[1][k][...] = (nn(gdel[k][...], both[0][k][...]) + nn(udel[k][...], both[1][k][...])).astype(BF)
        back3(1, k, bk3)

    d1, d2, d3 = ROUTES[0]
    cross_q.arrived()
    q = qbuf[...] + qsib[...]
    for i in range(4):
        rgsend[i] = q[:, i * 128 : i * 128 + 128]
    rg3 = remote.group(qrec.at[pl.ds(0, 3)])
    for j in (2, 1, 3):
        rg3.start(rgsend.at[at(d3, j)], qrec.at[c[d3]], peer(d3, j))
    qrec[c[d3]] = rgsend[c[d3]]

    out1 = [back1(0, k, out2[k]) for k in PARTS]

    rg3.arrived()
    rg3.sent()
    for c2 in range(4):
        ids, wts = table(0, c2)
        spots = jnp.concatenate([qrec[d][:, c2 * 32 : c2 * 32 + 32] for d in range(4)], axis=1)
        values = jnp.dot(
            jnp.where(sub8 == lane8, spots, 0.0),
            pick[0][pl.ds(c2 * 128, 128), :].astype(F32),
            precision=lax.Precision.HIGHEST,
            preferred_element_type=F32,
        )
        rg = jnp.zeros((8, 128), F32)
        for d in range(4):
            rg = rg + jnp.where(ids == expert_at(d3, d), values[d : d + 1, :], 0.0)
        rgsend[c2] = rg / wts
    rgc2 = remote.group(rg2)
    for j in (2, 1, 3):
        rgc2.start(rgsend.at[at(d2, j)], rg2.at[j - 1], peer(d2, j))

    bk2 = back2(1, bk3)
    rgc2.arrived()
    rg1send[...] = rgsend[c[d2]] + rg2[0] + rg2[1] + rg2[2]
    rgc1 = remote.group(rg1)
    for j in (2, 1, 3):
        rgc1.start(rg1send, rg1.at[j - 1], peer(d1, j))
    for k in PARTS:
        back0(0, k, out1[k], mixed)
    rgc1.arrived()
    rg = rg1send[...] + rg1[0] + rg1[1] + rg1[2]
    mine = rg[:, 0:32]
    for i in range(1, 4):
        mine = jnp.where(c[d1] == i, rg[:, i * 32 : i * 32 + 32], mine)
    rgo[...] = mine
    bk1 = [back1(1, k, bk2[k]) for k in PARTS]
    for i, dst in enumerate((t_out, g_out, h_out, gd_out, ud_out)):
        pltpu.make_async_copy(dst, dst, osems.at[i]).wait()
    for k in PARTS:
        back0(1, k, bk1[k], tgrad)
    remote.finish()


N_GROUPS = 94


def run_main(tok, og, ids, wts, gw, uw, dw):
    vm = pltpu.VMEM
    scratch = [vm((16, 128), F32)]

    def per(make):
        scratch.extend(make(WIDE[k]) for k in PARTS)

    for _ in range(8):
        per(lambda w: vm((512, w), BF))
    scratch.append(vm((3, 4, 4, 16, 128), F32))
    per(lambda w: vm((512, 128), BF))
    per(lambda w: vm((512, 128), BF))
    per(lambda w: vm((512, 1), F32))
    for _ in range(3):
        per(lambda w: vm((2 * HID, w), BF))
    for _ in range(3):
        per(lambda w: vm((HID, w), BF))
    per(lambda w: vm((512, HID), F32))
    scratch.extend(vm((512, HID), F32) for _ in range(4))
    for _ in range(3):
        per(lambda w: vm((512, 2 * HID), BF))
    scratch.extend(vm(s, F32) for s in ((8, 512), (8, 512), (4, 8, 128), (4, 8, 128), (3, 8, 128), (8, 128), (3, 8, 128)))
    for _ in range(2):
        per(lambda w: vm((512, w), BF))
    for _ in range(2):
        per(lambda w: vm((3, 128, w), BF))
    for _ in range(2):
        per(lambda w: vm((128, w), BF))
    for _ in range(2):
        per(lambda w: vm((3, 32, w), BF))
    scratch.extend(
        [
            pltpu.SemaphoreType.DMA((N_GROUPS,)),
            pltpu.SemaphoreType.DMA((N_GROUPS,)),
            pltpu.SemaphoreType.DMA((3,)),
            pltpu.SemaphoreType.DMA((5,)),
        ]
    )
    in_vmem = pl.BlockSpec(memory_space=pltpu.VMEM)
    anywhere = pl.BlockSpec(memory_space=pl.ANY)
    shape = jax.ShapeDtypeStruct
    return pl.pallas_call(
        main_kernel,
        out_shape=(
            shape((32, HALF), BF),
            shape((32, HALF), BF),
            shape((8, 32), F32),
            shape((512, 2 * HALF), BF),
            shape((512, 2 * HALF), BF),
            shape((3, 512, HID), BF),
            shape((3, 512, HID), BF),
            shape((3, 512, HID), BF),
        ),
        in_specs=[in_vmem] * 4 + [anywhere] * 3,
        out_specs=(in_vmem,) * 3 + (anywhere,) * 5,
        scratch_shapes=scratch,
        compiler_params=pltpu.CompilerParams(collective_id=0, has_side_effects=True, vmem_limit_bytes=63 * 2**20),
        cost_estimate=pl.CostEstimate(flops=10**10, bytes_accessed=2 * 10**7, transcendentals=10**6),
    )(tok, og, ids, wts, gw, uw, dw)


def grads_kernel(
    t_in, g_in, h_in, gd_in, ud_in, mixed_in, tgrad_in, rg_in,
    gg, ug, dg, mixed, tgrad, rg,
    tv, gv, hv, gdv, udv, ggv, ugv, dgv, lsems, csems, osems, psems
):
    passing = [
        pltpu.make_async_copy(src, dst, psems.at[i])
        for i, (src, dst) in enumerate(((mixed_in, mixed), (tgrad_in, tgrad), (rg_in, rg)))
    ]
    lefts, pairs = [], []
    for k in PARTS:
        lefts.append(
            [
                pltpu.make_async_copy(src.at[k], dst.at[k], lsems.at[k * 3 + i])
                for i, (src, dst) in enumerate(((gd_in, gdv), (ud_in, udv), (h_in, hv)))
            ]
        )
        for copy in lefts[k]:
            copy.start()
        for half in range(2):
            cols = pl.ds(half * HALF + FROM[k], WIDE[k])
            at = (k * 2 + half) * 2
            pair = [
                pltpu.make_async_copy(t_in.at[:, cols], tv.at[:, cols], csems.at[at]),
                pltpu.make_async_copy(g_in.at[:, cols], gv.at[:, cols], csems.at[at + 1]),
            ]
            for copy in pair:
                copy.start()
            pairs.append(pair)
    for copy in passing:
        copy.start()
    outs = []
    for k in PARTS:
        for copy in lefts[k]:
            copy.wait()
        pair_t = jnp.concatenate([gdv[k].T, udv[k].T], axis=0)
        hid_t = hv[k].T
        for half in range(2):
            cols = pl.ds(half * HALF + FROM[k], WIDE[k])
            for copy in pairs[k * 2 + half]:
                copy.wait()
            two = nn(pair_t, tv[:, cols]).astype(BF)
            ggv[:, cols] = two[:HID]
            ugv[:, cols] = two[HID:]
            dgv[:, cols] = nn(hid_t, gv[:, cols]).astype(BF)
            for mid, dst in zip((ggv, ugv, dgv), (gg, ug, dg)):
                out = pltpu.make_async_copy(mid.at[:, cols], dst.at[0, :, cols], osems.at[len(outs)])
                out.start()
                outs.append(out)
    for out in outs + passing:
        out.wait()


def run_grads(t_rows, g_rows, h, gd, ud, mixed, tgrad, rg):
    anywhere = pl.BlockSpec(memory_space=pl.ANY)
    vm = pltpu.VMEM
    dma = pltpu.SemaphoreType.DMA
    shape = jax.ShapeDtypeStruct
    return pl.pallas_call(
        grads_kernel,
        out_shape=(shape((1, HID, 2 * HALF), BF),) * 3
        + tuple(shape(x.shape, x.dtype) for x in (mixed, tgrad, rg)),
        in_specs=[anywhere] * 8,
        out_specs=(anywhere,) * 6,
        scratch_shapes=[vm((512, 2 * HALF), BF)] * 2
        + [vm((3, 512, HID), BF)] * 3
        + [vm((HID, 2 * HALF), BF)] * 3
        + [dma((9,)), dma((12,)), dma((18,)), dma((3,))],
        compiler_params=pltpu.CompilerParams(vmem_limit_bytes=62 * 2**20),
        cost_estimate=pl.CostEstimate(flops=5 * 10**9, bytes_accessed=2 * 10**7, transcendentals=0),
    )(t_rows, g_rows, h, gd, ud, mixed, tgrad, rg)


def shards(tokens, route_ids, route_weight, gate_weight, up_weight, down_weight, out_grad):
    mixed, tgrad, rg, t_rows, g_rows, h, gd, ud = run_main(
        tokens, out_grad, route_ids.T, route_weight.T, gate_weight, up_weight, down_weight
    )
    gate_grad, up_grad, down_grad, mixed, tgrad, rg = run_grads(t_rows, g_rows, h, gd, ud, mixed, tgrad, rg)
    return (mixed, tgrad, rg.T, gate_grad, up_grad, down_grad)


def solution(mesh):
    placed = (
        P("expert", "tensor"),
        P("expert", None),
        P("expert", None),
        P("expert", "tensor", None),
        P("expert", "tensor", None),
        P("expert", "tensor", None),
        P("expert", "tensor"),
    )
    return jax.shard_map(
        shards,
        mesh=mesh,
        in_specs=placed,
        out_specs=(
            P("expert", "tensor"),
            P("expert", "tensor"),
            P("expert", None),
            P("expert", "tensor", None),
            P("expert", "tensor", None),
            P("expert", "tensor", None),
        ),
        check_vma=False,
    )
```
